512 devices in a mesh: row: 32 (over x, y, core), col: 16 (over z).
Axes of the slice: x: 4, y: 4, z: 16, core: 2. Of those that a mesh axis runs over, the one named last changes fastest.
Arguments:
- vectors: float32 [2, 128, 128, 8192], P(None, 'row', None, 'col'), may hold values from -120 to 120
- potential: int32 [4, 128, 128], replicated, may hold values from 0 to 4095
Outputs:
- renewed: float32 [2, 128, 128, 8192], P(None, 'row', None, 'col')
- growth: float32 [8192], P('col')
The draws below stay inside these ranges and needn't reach their ends.
All inputs are finite; a program needn't handle non-finite values.
Results may differ from the reference program's by a relative error of at most 0.00016.
Values sent between devices are 32-bit elements; how exact they have to be, the bound alone decides.
No kernel may reach another device: no remote copies, remote signals or barrier semaphores. Data moves between devices by JAX's collectives and lax.ppermute only.
A program may use at most 64 MiB of HBM per device.

```python
import math
import jax
import jax.numpy as jnp
from jax import lax

MX = 128
MY = 128
SLICES = 4
PANEL = 128
PANELS = 2
LEVELS = 4096
COLS_DEV = 512
VECTORS = 8192
ROWS = 32768


def draw_vectors(key, part):
    key = jax.random.fold_in(key, 11)
    base_key, column_key = jax.random.split(key, 2)
    rows = jnp.arange(MX).astype(jnp.float32)
    row_scale = jnp.exp(math.log(3.0) * rows / (MX - 1))
    column_scale = jnp.exp(jax.random.uniform(column_key, (VECTORS,), jnp.float32, 0.0, math.log(10.0)))
    values = jnp.clip(jax.random.normal(base_key, (2, MX, MY, VECTORS), jnp.float32), -4.0, 4.0)
    return values * row_scale[None, :, None, None] * column_scale


def place_ends(values, key, smallest, top_value):
    place = [jax.random.randint(jax.random.fold_in(key, axis), (), 0, length) for axis, length in enumerate(values.shape)]
    widest = values.shape.index(max(values.shape))
    beside = place[:widest] + [(place[widest] + 1) % values.shape[widest]] + place[widest + 1:]
    return values.at[tuple(place)].set(smallest).at[tuple(beside)].set(top_value)


def setup_inputs(seed: int = 0) -> dict:
    splits = jax.random.split(jax.random.key(seed), 3)
    return {
        "vectors": draw_vectors(jax.random.fold_in(splits[2], 71), 0),
        "potential": place_ends(jax.random.randint(splits[1], (SLICES, MX, MY), 0, LEVELS), jax.random.fold_in(splits[1], 1), 0, LEVELS - 1).astype(jnp.int32),
    }


energy = 0.25
disorder = 16.5
tiny = 1e-06
highest = lax.Precision.HIGHEST

def site_values(codes):
    return disorder * ((codes.astype(jnp.float32) + 0.5) / LEVELS - 0.5)

def contract(left, right):
    return lax.dot_general(left.astype(jnp.float32), right.astype(jnp.float32), (((0,), (0,)), ((), ())), precision=highest, preferred_element_type=jnp.float32)

def reference(vectors, potential):
    values = site_values(potential)
    current = vectors[0]
    previous = vectors[1]
    for step in range(SLICES):
        beside = jnp.roll(current, 1, axis=0) + jnp.roll(current, -1, axis=0)
        beside = beside + jnp.roll(current, 1, axis=1) + jnp.roll(current, -1, axis=1)
        fresh = (energy - values[step][:, :, None]) * current - beside - previous
        previous = current
        current = fresh
    matrix = jnp.stack([current, previous]).reshape(ROWS, VECTORS)
    squares = lax.optimization_barrier(jnp.sum(matrix * matrix, 0))
    scale = jnp.sqrt(squares / ROWS + tiny)
    growth = jnp.log(scale)
    matrix = matrix / scale
    columns = jnp.arange(VECTORS)
    within = columns % COLS_DEV < PANEL
    for panel in range(PANELS):
        start = panel * COLS_DEV
        raw = matrix[:, start:start + PANEL]
        gram = contract(raw, raw) / ROWS
        lower = jnp.linalg.cholesky(gram)
        basis = lax.linalg.triangular_solve(lower, raw, left_side=False, lower=True, transpose_a=True)
        coeffs = contract(basis, matrix) / ROWS
        update = matrix - jnp.dot(basis.astype(jnp.float32), coeffs.astype(jnp.float32), precision=highest, preferred_element_type=jnp.float32)
        keep = within & (columns // COLS_DEV <= panel)
        matrix = jnp.where(keep[None, :], matrix, update)
        matrix = matrix.at[:, start:start + PANEL].set(basis)
    return (matrix.reshape(2, MX, MY, VECTORS), growth)
```

```python
import functools

import jax
import jax.numpy as jnp
from jax import lax
from jax.experimental import pallas as pl
from jax.experimental.pallas import tpu as pltpu
from jax.sharding import PartitionSpec as P

PANEL = 128
LEVELS = 4096
BLOCK = 128

energy = 0.25
disorder = 16.5
tiny = 1e-06
highest = lax.Precision.HIGHEST
MIB = 2**20


def site_values(codes):
    return disorder * ((codes.astype(jnp.float32) + 0.5) / LEVELS - 0.5)


def dot(left, right, contract):
    return lax.dot_general(
        left, right, ((contract[:1], contract[1:]), ((), ())),
        precision=highest, preferred_element_type=jnp.float32,
    )


def stencil_kernel(depth, vec_ref, low_ref, high_ref, coef_ref, out_ref, a_ref, b_ref):
    rows = vec_ref.shape[1]
    for i in range(rows):
        a_ref[i] = low_ref[i]
        a_ref[rows + i] = vec_ref[0, i]
        a_ref[2 * rows + i] = high_ref[i]
        b_ref[rows + i] = vec_ref[1, i]
    for i in range(depth - 1):
        b_ref[rows - depth + 1 + i] = low_ref[rows + i]
        b_ref[2 * rows + i] = high_ref[rows + i]
    current, previous = a_ref, b_ref
    sites = vec_ref.shape[2]
    for step in range(depth):
        reach = depth - 1 - step

        def one_row(i, _, current=current, previous=previous, step=step):
            center = current[i]
            beside = current[i + 1] + current[i - 1]
            beside = beside + pltpu.roll(center, 1, 0) + pltpu.roll(center, sites - 1, 0)
            previous[i] = coef_ref[step, i - rows + depth - 1] * center - beside - previous[i]
            return 0

        lax.fori_loop(rows - reach, 2 * rows + reach, one_row, 0)
        current, previous = previous, current
    for i in range(rows):
        out_ref[0, i] = current[rows + i]
        out_ref[1, i] = previous[rows + i]


def stencil(vectors, low, high, coefs, first, count):
    _, rows, sites, _ = vectors.shape
    depth = coefs.shape[0]
    halo = low.shape[0]
    return pl.pallas_call(
        functools.partial(stencil_kernel, depth),
        grid=(count,),
        in_specs=[
            pl.BlockSpec((2, rows, sites, BLOCK), lambda i: (0, 0, 0, i + first)),
            pl.BlockSpec((halo, sites, BLOCK), lambda i: (0, 0, i)),
            pl.BlockSpec((halo, sites, BLOCK), lambda i: (0, 0, i)),
            pl.BlockSpec(coefs.shape, lambda i: (0, 0, 0, 0)),
        ],
        out_specs=pl.BlockSpec((2, rows, sites, BLOCK), lambda i: (0, 0, 0, i)),
        out_shape=jax.ShapeDtypeStruct((2, rows, sites, count * BLOCK), jnp.float32),
        scratch_shapes=[
            pltpu.VMEM((3 * rows, sites, BLOCK), jnp.float32),
            pltpu.VMEM((3 * rows, sites, BLOCK), jnp.float32),
        ],
        compiler_params=pltpu.CompilerParams(vmem_limit_bytes=40 * MIB),
        name="slices",
    )(vectors, low, high, coefs)


def eliminate(mat_ref, inv_ref, first, last):
    size = mat_ref.shape[0]
    lanes = lax.broadcasted_iota(jnp.int32, (size, size), 1)
    subs = lax.broadcasted_iota(jnp.int32, (size, size), 0)

    def one_column(j, _):
        mat = mat_ref[...]
        row = mat_ref[pl.ds(j, 1), :]
        inv_row = inv_ref[pl.ds(j, 1), :]
        pivot = jnp.sum(jnp.where(lanes[:1] == j, row, 0.0), axis=1, keepdims=True)
        column = jnp.sum(jnp.where(lanes == j, mat, 0.0), axis=1, keepdims=True)
        factor = jnp.where(subs[:, :1] > j, column * (1.0 / pivot), 0.0)
        mat_ref[...] = mat - factor * row
        inv_ref[...] = inv_ref[...] - factor * inv_row
        inv_ref[pl.ds(j, 1), :] = inv_row * lax.rsqrt(pivot)
        return 0

    lax.fori_loop(first, last, one_column, 0)


def identity(size):
    lanes = lax.broadcasted_iota(jnp.int32, (size, size), 1)
    subs = lax.broadcasted_iota(jnp.int32, (size, size), 0)
    return jnp.where(lanes == subs, 1.0, 0.0).astype(jnp.float32)


def block_scales(block, total):
    diag = identity(PANEL) * block
    along = lax.rsqrt(jnp.sum(diag, axis=0, keepdims=True) / total + tiny)
    down = lax.rsqrt(jnp.sum(diag, axis=1, keepdims=True) / total + tiny)
    return along, down


def start_kernel(total, pack_ref, mat_ref, inv_ref):
    block = pack_ref[0:PANEL]
    along, down = block_scales(block, total)
    mat_ref[...] = block * down * along / total
    inv_ref[...] = identity(PANEL)
    eliminate(mat_ref, inv_ref, 0, PANEL // 2)


def middle_kernel(total, pack_ref, mat_in, inv_in, rest_ref, inv_ref, cross_ref, mat_ref):
    mat_ref[...] = mat_in[...]
    inv_ref[...] = inv_in[...]
    eliminate(mat_ref, inv_ref, PANEL // 2, PANEL)
    _, down0 = block_scales(pack_ref[0:PANEL], total)
    block = pack_ref[2 * PANEL:3 * PANEL]
    along1, down1 = block_scales(block, total)
    cross = dot(inv_ref[...], pack_ref[PANEL:2 * PANEL] * down0 * along1 / total, (1, 0))
    cross_ref[...] = cross
    rest_ref[...] = block * down1 * along1 / total - dot(cross, cross, (0, 0))


def next_kernel(rest_ref, mat_ref, inv_ref):
    mat_ref[...] = rest_ref[...]
    inv_ref[...] = identity(PANEL)
    eliminate(mat_ref, inv_ref, 0, PANEL // 2)


def finish_kernel(total, pack_ref, inv0_ref, cross_ref, mat_in, inv_in, out_ref, mat_ref, inv_ref):
    mat_ref[...] = mat_in[...]
    inv_ref[...] = inv_in[...]
    eliminate(mat_ref, inv_ref, PANEL // 2, PANEL)
    along0, _ = block_scales(pack_ref[0:PANEL], total)
    along1, _ = block_scales(pack_ref[2 * PANEL:3 * PANEL], total)
    inv0 = inv0_ref[...]
    inv1 = inv_ref[...]
    mixed = -dot(dot(inv1, cross_ref[...], (1, 1)), inv0, (1, 0))
    out_ref[0:PANEL, 0:PANEL] = inv0 * along0
    out_ref[0:PANEL, PANEL:] = jnp.zeros((PANEL, PANEL), jnp.float32)
    out_ref[PANEL:, 0:PANEL] = mixed * along0
    out_ref[PANEL:, PANEL:] = inv1 * along1


def call(kernel, name, outs, scratch, *args):
    square = pltpu.VMEM((PANEL, PANEL), jnp.float32)
    shapes = [jax.ShapeDtypeStruct((k * PANEL, k * PANEL), jnp.float32) for k in outs]
    return pl.pallas_call(
        kernel,
        out_shape=shapes,
        scratch_shapes=[square] * scratch,
        compiler_params=pltpu.CompilerParams(vmem_limit_bytes=16 * MIB),
        cost_estimate=pl.CostEstimate(flops=2 * 10**9, bytes_accessed=10**6, transcendentals=0),
        name=name,
    )(*args)


def factor(pack, total):
    mat, inv = call(functools.partial(start_kernel, total), "factor_a", [1, 1], 0, pack)
    rest, inv0, cross = call(functools.partial(middle_kernel, total), "factor_b", [1, 1, 1], 1, pack, mat, inv)
    mat, inv = call(next_kernel, "factor_c", [1, 1], 0, rest)
    out, = call(functools.partial(finish_kernel, total), "factor_d", [2], 2, pack, inv0, cross, mat, inv)
    return out


def on_device(vectors, potential):
    depth = potential.shape[0]
    _, rows, sites, columns = vectors.shape
    row_count = lax.axis_size("row")
    row_index = lax.axis_index("row")
    col_index = lax.axis_index("col")
    total = 2 * rows * sites * row_count

    forward = [(i, (i + 1) % row_count) for i in range(row_count)]
    backward = [(target, source) for source, target in forward]

    def halos(first, last):
        current = vectors[0, :, :, first:last]
        previous = vectors[1, :, :, first:last]
        up = jnp.concatenate([current, previous[rows - depth + 1:]], 0)
        down = jnp.concatenate([current, previous[:depth - 1]], 0)
        return lax.ppermute(up, "row", forward), lax.ppermute(down, "row", backward)

    low_panel, high_panel = halos(0, PANEL)
    low_rest, high_rest = halos(PANEL, columns)
    site_rows = (row_index * rows - depth + 1 + jnp.arange(rows + 2 * depth - 2)) % potential.shape[1]
    coefs = energy - site_values(jnp.take(potential, site_rows, axis=1))
    coefs = jnp.broadcast_to(coefs[..., None], coefs.shape + (BLOCK,))

    own = stencil(vectors, low_panel, high_panel, coefs, 0, 1)
    rest = stencil(vectors, low_rest, high_rest, coefs, 1, columns // BLOCK - 1)
    own = own.reshape(-1, PANEL)
    matrix = jnp.concatenate([own, rest.reshape(own.shape[0], -1)], 1)

    held = jnp.where(col_index < 2, own, 0.0)
    stages = [
        [(0, 9), (1, 8)],
        [(0, 4), (8, 12), (1, 13), (9, 5)],
        [(1, 3), (13, 15), (5, 7), (9, 11), (4, 2), (0, 14), (8, 6), (12, 10)],
    ]
    for pairs in stages:
        held = held + lax.ppermute(held, "col", pairs)
    pairs = [(4, 3), (2, 1), (0, 15), (14, 13), (12, 11), (10, 9), (8, 7), (6, 5)]
    other = lax.ppermute(held, "col", pairs + [(b, a) for a, b in pairs])
    has_first = functools.reduce(jnp.logical_or, [col_index == c for c in (0, 2, 4, 5, 7, 9, 11, 14)])
    panel0 = jnp.where(has_first, held, other)
    panel1 = jnp.where(has_first, other, held)
    panels = jnp.concatenate([panel0, panel1], 1)

    products = dot(panels, panels, (0, 0))
    coeffs = dot(panels, matrix, (0, 0))
    squares = jnp.sum(matrix * matrix, 0).reshape(-1, BLOCK)
    small = jnp.concatenate([
        products[:PANEL, :PANEL],
        products[:PANEL, PANEL:],
        products[PANEL:, PANEL:],
        jnp.pad(squares, ((0, PANEL - squares.shape[0]), (0, 0))),
    ], 0)
    large = jnp.moveaxis(coeffs.reshape(2 * PANEL, -1, BLOCK), 1, 0).reshape(-1, BLOCK)

    def shares(array):
        return array.reshape(row_count, -1, BLOCK)

    def scattered(array):
        return jnp.sum(lax.all_to_all(array, "row", 0, 0), 0)

    def gathered(array):
        everywhere = jnp.broadcast_to(array, (row_count,) + array.shape)
        return lax.all_to_all(everywhere, "row", 0, 0).reshape(-1, BLOCK)

    share = scattered(jnp.concatenate([shares(small), shares(large)], 1))
    cut = small.shape[0] // row_count
    small = gathered(share[:cut])
    inverse = factor(small, total)
    large = gathered(share[cut:])

    coeffs = jnp.moveaxis(large.reshape(-1, 2 * PANEL, BLOCK), 0, 1).reshape(2 * PANEL, -1)
    squares = small[3 * PANEL:3 * PANEL + columns // BLOCK].reshape(-1)
    scale = jnp.sqrt(squares / total + tiny)
    growth = jnp.log(scale)
    weights = dot(inverse, dot(inverse, coeffs, (1, 0)), (0, 0)) / total
    basis = jnp.where(col_index == 0, inverse[:PANEL], inverse[PANEL:])
    holder = col_index < 2
    first = jnp.where(holder, -basis.T, weights[:, :PANEL])
    weights = jnp.concatenate([first, weights[:, PANEL:]], 1)
    is_panel = holder & (jnp.arange(columns) < PANEL)
    keep = jnp.where(is_panel, 0.0, 1.0)
    shrink = jnp.where(is_panel, 1.0, 1.0 / scale)
    result = (matrix * keep - dot(panels, weights, (1, 0))) * shrink
    return (result.reshape(vectors.shape), growth)


def solution(mesh):
    return jax.shard_map(
        on_device,
        mesh=mesh,
        in_specs=(P(None, "row", None, "col"), P()),
        out_specs=(P(None, "row", None, "col"), P("col")),
        check_vma=False,
    )
```

```python
import functools

import jax
import jax.numpy as jnp
from jax import lax
from jax.experimental import pallas as pl
from jax.experimental.pallas import tpu as pltpu
from jax.sharding import PartitionSpec as P

PANEL = 128
LEVELS = 4096
BLOCK = 128

energy = 0.25
disorder = 16.5
tiny = 1e-06
highest = lax.Precision.HIGHEST
MIB = 2**20


def site_values(codes):
    return disorder * ((codes.astype(jnp.float32) + 0.5) / LEVELS - 0.5)


def dot(left, right, contract):
    return lax.dot_general(
        left, right, ((contract[:1], contract[1:]), ((), ())),
        precision=highest, preferred_element_type=jnp.float32,
    )


def stencil_kernel(depth, vec_ref, low_ref, high_ref, coef_ref, out_ref, a_ref, b_ref):
    rows = vec_ref.shape[1]
    for i in range(rows):
        a_ref[i] = low_ref[i]
        a_ref[rows + i] = vec_ref[0, i]
        a_ref[2 * rows + i] = high_ref[i]
        b_ref[rows + i] = vec_ref[1, i]
    for i in range(depth - 1):
        b_ref[rows - depth + 1 + i] = low_ref[rows + i]
        b_ref[2 * rows + i] = high_ref[rows + i]
    current, previous = a_ref, b_ref
    sites = vec_ref.shape[2]
    for step in range(depth):
        reach = depth - 1 - step

        def one_row(i, _, current=current, previous=previous, step=step):
            center = current[i]
            beside = current[i + 1] + current[i - 1]
            beside = beside + pltpu.roll(center, 1, 0) + pltpu.roll(center, sites - 1, 0)
            previous[i] = coef_ref[step, i - rows + depth - 1] * center - beside - previous[i]
            return 0

        lax.fori_loop(rows - reach, 2 * rows + reach, one_row, 0)
        current, previous = previous, current
    for i in range(rows):
        out_ref[0, i] = current[rows + i]
        out_ref[1, i] = previous[rows + i]


def stencil(vectors, low, high, coefs, first, count):
    _, rows, sites, _ = vectors.shape
    depth = coefs.shape[0]
    halo = low.shape[0]
    return pl.pallas_call(
        functools.partial(stencil_kernel, depth),
        grid=(count,),
        in_specs=[
            pl.BlockSpec((2, rows, sites, BLOCK), lambda i: (0, 0, 0, i + first)),
            pl.BlockSpec((halo, sites, BLOCK), lambda i: (0, 0, i)),
            pl.BlockSpec((halo, sites, BLOCK), lambda i: (0, 0, i)),
            pl.BlockSpec(coefs.shape, lambda i: (0, 0, 0, 0)),
        ],
        out_specs=pl.BlockSpec((2, rows, sites, BLOCK), lambda i: (0, 0, 0, i)),
        out_shape=jax.ShapeDtypeStruct((2, rows, sites, count * BLOCK), jnp.float32),
        scratch_shapes=[
            pltpu.VMEM((3 * rows, sites, BLOCK), jnp.float32),
            pltpu.VMEM((3 * rows, sites, BLOCK), jnp.float32),
        ],
        compiler_params=pltpu.CompilerParams(vmem_limit_bytes=40 * MIB),
        name="slices",
    )(vectors, low, high, coefs)


def eliminate(mat_ref, inv_ref):
    size = mat_ref.shape[0]
    step = 8
    wide = (step, 2 * size)
    lanes = lax.broadcasted_iota(jnp.int32, (step, size), 1)
    subs = lax.broadcasted_iota(jnp.int32, wide, 0)
    inv_ref[...] = identity(size)
    for first in range(0, size, step):
        last = first + step
        both = jnp.concatenate([mat_ref[first:last], inv_ref[first:last]], 1)
        columns = [jnp.broadcast_to(both[:, first + k:first + k + 1], (step, size)) for k in range(step)]
        entry = [[jnp.broadcast_to(columns[k][i:i + 1], (step, size)) for k in range(i + 1)] for i in range(step)]
        rows = [jnp.broadcast_to(both[i:i + 1], wide) for i in range(step)]
        result = jnp.zeros(wide, jnp.float32)
        for k in range(step):
            root = lax.rsqrt(entry[k][k])
            done = rows[k] * jnp.concatenate([root, root], 1)
            result = jnp.where(subs == k, done, result)
            lower = {i: entry[i][k] * root for i in range(k + 1, step)}
            for i in range(k + 1, step):
                for j in range(k + 1, i + 1):
                    entry[i][j] = entry[i][j] - lower[i] * lower[j]
                rows[i] = rows[i] - jnp.concatenate([lower[i], lower[i]], 1) * done
        inv_ref[first:last] = result[:, size:]
        if last < size:
            below = jnp.where(lanes >= last, result[:, :size], 0.0)
            change = dot(below, result, (0, 0))
            mat_ref[last:] = mat_ref[last:] - change[last:, :size]
            inv_ref[last:] = inv_ref[last:] - change[last:, size:]


def identity(size):
    lanes = lax.broadcasted_iota(jnp.int32, (size, size), 1)
    subs = lax.broadcasted_iota(jnp.int32, (size, size), 0)
    return jnp.where(lanes == subs, 1.0, 0.0).astype(jnp.float32)


def block_scales(block, total):
    diag = identity(PANEL) * block
    along = lax.rsqrt(jnp.sum(diag, axis=0, keepdims=True) / total + tiny)
    down = lax.rsqrt(jnp.sum(diag, axis=1, keepdims=True) / total + tiny)
    return along, down


def first_kernel(total, pack_ref, rest_ref, inv_ref, cross_ref, mat_ref):
    block = pack_ref[0:PANEL]
    along0, down0 = block_scales(block, total)
    mat_ref[...] = block * down0 * along0 / total
    eliminate(mat_ref, inv_ref)
    block = pack_ref[2 * PANEL:3 * PANEL]
    along1, down1 = block_scales(block, total)
    cross = dot(inv_ref[...], pack_ref[PANEL:2 * PANEL] * down0 * along1 / total, (1, 0))
    cross_ref[...] = cross
    rest_ref[...] = block * down1 * along1 / total - dot(cross, cross, (0, 0))


def second_kernel(total, pack_ref, rest_ref, inv0_ref, cross_ref, out_ref, mat_ref, inv_ref):
    mat_ref[...] = rest_ref[...]
    eliminate(mat_ref, inv_ref)
    along0, _ = block_scales(pack_ref[0:PANEL], total)
    along1, _ = block_scales(pack_ref[2 * PANEL:3 * PANEL], total)
    inv0 = inv0_ref[...]
    inv1 = inv_ref[...]
    mixed = -dot(dot(inv1, cross_ref[...], (1, 1)), inv0, (1, 0))
    out_ref[0:PANEL, 0:PANEL] = inv0 * along0
    out_ref[0:PANEL, PANEL:] = jnp.zeros((PANEL, PANEL), jnp.float32)
    out_ref[PANEL:, 0:PANEL] = mixed * along0
    out_ref[PANEL:, PANEL:] = inv1 * along1


def call(kernel, name, outs, scratch, *args):
    square = pltpu.VMEM((PANEL, PANEL), jnp.float32)
    shapes = [jax.ShapeDtypeStruct((k * PANEL, k * PANEL), jnp.float32) for k in outs]
    return pl.pallas_call(
        kernel,
        out_shape=shapes,
        scratch_shapes=[square] * scratch,
        compiler_params=pltpu.CompilerParams(vmem_limit_bytes=16 * MIB),
        cost_estimate=pl.CostEstimate(flops=2 * 10**9, bytes_accessed=10**6, transcendentals=0),
        name=name,
    )(*args)


def factor(pack, total):
    rest, inv0, cross = call(functools.partial(first_kernel, total), "factor_a", [1, 1, 1], 1, pack)
    out, = call(functools.partial(second_kernel, total), "factor_b", [2], 2, pack, rest, inv0, cross)
    return out


def finish_kernel(total, place_ref, inv_ref, coef_ref, squares_ref, panel0_ref, panel1_ref, own_ref, rest_ref, out_ref):
    i = pl.program_id(0)
    place = place_ref[0]
    is_panel = jnp.logical_and(i == 0, place < 2)
    inverse = inv_ref[...]
    part = dot(inverse, coef_ref[...], (1, 0)) / total
    subs = lax.broadcasted_iota(jnp.int32, part.shape, 0)
    lanes = lax.broadcasted_iota(jnp.int32, part.shape, 1)
    chosen = jnp.where(subs == lanes + place * PANEL, -1.0, 0.0)
    part = jnp.where(is_panel, chosen, part)
    weights = dot(inverse, part, (0, 0))
    taken = dot(panel0_ref[...], weights[:PANEL], (1, 0)) + dot(panel1_ref[...], weights[PANEL:], (1, 0))
    block = jnp.where(i == 0, own_ref[...], rest_ref[...]).reshape(taken.shape)
    squares = squares_ref[pl.ds(i, 1), :]
    shrink = 1.0 / jnp.sqrt(squares / total + tiny)
    keep = jnp.where(is_panel, 0.0, 1.0)
    shrink = jnp.where(is_panel, 1.0, shrink)
    out_ref[...] = ((block * keep - taken) * shrink).reshape(out_ref.shape)


def finish(col_index, inverse, large, squares, panel0, panel1, own, rest, total):
    _, rows, sites, _ = own.shape
    count = rest.shape[3] // BLOCK + 1
    shape = (2, rows, sites, BLOCK)
    fixed = lambda array: pl.BlockSpec(array.shape, lambda i: (0,) * array.ndim)
    return pl.pallas_call(
        functools.partial(finish_kernel, total),
        grid=(count,),
        in_specs=[
            pl.BlockSpec(memory_space=pltpu.SMEM),
            fixed(inverse),
            pl.BlockSpec((2 * PANEL, BLOCK), lambda i: (i, 0)),
            fixed(squares),
            fixed(panel0),
            fixed(panel1),
            fixed(own),
            pl.BlockSpec(shape, lambda i: (0, 0, 0, jnp.maximum(i - 1, 0))),
        ],
        out_specs=pl.BlockSpec(shape, lambda i: (0, 0, 0, i)),
        out_shape=jax.ShapeDtypeStruct((2, rows, sites, count * BLOCK), jnp.float32),
        compiler_params=pltpu.CompilerParams(vmem_limit_bytes=40 * MIB),
        name="finish",
    )(col_index.reshape(1), inverse, large, squares, panel0, panel1, own, rest)


def on_device(vectors, potential):
    depth = potential.shape[0]
    _, rows, sites, columns = vectors.shape
    row_count = lax.axis_size("row")
    row_index = lax.axis_index("row")
    col_index = lax.axis_index("col")
    total = 2 * rows * sites * row_count

    forward = [(i, (i + 1) % row_count) for i in range(row_count)]
    backward = [(target, source) for source, target in forward]

    def halos(first, last):
        current = vectors[0, :, :, first:last]
        previous = vectors[1, :, :, first:last]
        up = jnp.concatenate([current, previous[rows - depth + 1:]], 0)
        down = jnp.concatenate([current, previous[:depth - 1]], 0)
        return lax.ppermute(up, "row", forward), lax.ppermute(down, "row", backward)

    low_panel, high_panel = halos(0, PANEL)
    low_rest, high_rest = halos(PANEL, columns)
    site_rows = (row_index * rows - depth + 1 + jnp.arange(rows + 2 * depth - 2)) % potential.shape[1]
    coefs = energy - site_values(jnp.take(potential, site_rows, axis=1))
    coefs = jnp.broadcast_to(coefs[..., None], coefs.shape + (BLOCK,))

    own = stencil(vectors, low_panel, high_panel, coefs, 0, 1)
    rest = stencil(vectors, low_rest, high_rest, coefs, 1, columns // BLOCK - 1)
    panel = own.reshape(-1, PANEL)
    matrix = jnp.concatenate([panel, rest.reshape(panel.shape[0], -1)], 1)

    stages = [
        [(0, 9), (1, 8)],
        [(0, 4), (8, 12), (1, 13), (9, 5)],
        [(1, 3), (13, 15), (5, 7), (9, 11), (4, 2), (0, 14), (8, 6), (12, 10)],
    ]

    def spread(array):
        array = jnp.where(col_index < 2, array, 0.0)
        for pairs in stages:
            array = array + lax.ppermute(array, "col", pairs)
        return array

    def scattered(array):
        return jnp.sum(lax.all_to_all(array.reshape(row_count, -1, BLOCK), "row", 0, 0), 0)

    def gathered(array):
        everywhere = jnp.broadcast_to(array, (row_count,) + array.shape)
        return lax.all_to_all(everywhere, "row", 0, 0)

    swapped = lax.ppermute(panel, "col", [(0, 1), (1, 0)])
    first = jnp.where(col_index == 0, panel, swapped)
    second = jnp.where(col_index == 0, swapped, panel)
    products = jnp.concatenate([
        dot(first, first, (0, 0)),
        dot(first, second, (0, 0)),
        dot(second, second, (0, 0)),
        jnp.zeros((PANEL, PANEL), jnp.float32),
    ], 0)
    inverse = factor(gathered(spread(scattered(products))).reshape(-1, BLOCK), total)

    held = spread(panel)
    pairs = [(4, 3), (2, 1), (0, 15), (14, 13), (12, 11), (10, 9), (8, 7), (6, 5)]
    other = lax.ppermute(held, "col", pairs + [(b, a) for a, b in pairs])
    has_first = functools.reduce(jnp.logical_or, [col_index == c for c in (0, 2, 4, 5, 7, 9, 11, 14)])
    panel0 = jnp.where(has_first, held, other)
    panel1 = jnp.where(has_first, other, held)

    coeffs = dot(jnp.concatenate([panel0, panel1], 1), matrix, (0, 0))
    large = jnp.moveaxis(coeffs.reshape(2 * PANEL, -1, BLOCK), 1, 0).reshape(row_count, -1, BLOCK)
    squares = jnp.sum(matrix * matrix, 0).reshape(-1, BLOCK)
    squares = jnp.pad(squares, ((0, 8 * row_count - squares.shape[0]), (0, 0)))
    cut = large.shape[1]
    share = scattered(jnp.concatenate([large, squares.reshape(row_count, 8, BLOCK)], 1))
    every = gathered(share)
    large = every[:, :cut].reshape(-1, BLOCK)
    squares = every[0, cut:]
    result = finish(col_index, inverse, large, squares, panel0, panel1, own, rest, total)
    scale = jnp.sqrt(squares[:columns // BLOCK].reshape(-1) / total + tiny)
    return (result, jnp.log(scale))


def solution(mesh):
    return jax.shard_map(
        on_device,
        mesh=mesh,
        in_specs=(P(None, "row", None, "col"), P()),
        out_specs=(P(None, "row", None, "col"), P("col")),
        check_vma=False,
    )
```

```python
import functools

import jax
import jax.numpy as jnp
from jax import lax
from jax.experimental import pallas as pl
from jax.experimental.pallas import tpu as pltpu
from jax.sharding import PartitionSpec as P

PANEL = 128
LEVELS = 4096
BLOCK = 128
SMALL = 16

energy = 0.25
disorder = 16.5
tiny = 1e-06
highest = lax.Precision.HIGHEST
MIB = 2**20


def site_values(codes):
    return disorder * ((codes.astype(jnp.float32) + 0.5) / LEVELS - 0.5)


def dot(left, right, contract):
    return lax.dot_general(
        left, right, ((contract[:1], contract[1:]), ((), ())),
        precision=highest, preferred_element_type=jnp.float32,
    )


def stencil_kernel(depth, vec_ref, low_ref, high_ref, coef_ref, out_ref, a_ref, b_ref):
    rows = vec_ref.shape[1]
    for i in range(rows):
        a_ref[i] = low_ref[0, i]
        a_ref[rows + i] = vec_ref[0, i]
        a_ref[2 * rows + i] = high_ref[0, i]
        b_ref[i] = low_ref[1, i]
        b_ref[rows + i] = vec_ref[1, i]
        b_ref[2 * rows + i] = high_ref[1, i]
    current, previous = a_ref, b_ref
    sites = vec_ref.shape[2]
    for step in range(depth):
        reach = depth - 1 - step

        def one_row(i, _, current=current, previous=previous, step=step):
            center = current[i]
            beside = current[i + 1] + current[i - 1]
            beside = beside + pltpu.roll(center, 1, 0) + pltpu.roll(center, sites - 1, 0)
            previous[i] = coef_ref[step, i - rows + depth - 1] * center - beside - previous[i]
            return 0

        lax.fori_loop(rows - reach, 2 * rows + reach, one_row, 0)
        current, previous = previous, current
    for i in range(rows):
        out_ref[0, i] = current[rows + i]
        out_ref[1, i] = previous[rows + i]


def stencil(vectors, low, high, coefs):
    _, rows, sites, columns = vectors.shape
    block = pl.BlockSpec((2, rows, sites, BLOCK), lambda i: (0, 0, 0, i))
    return pl.pallas_call(
        functools.partial(stencil_kernel, coefs.shape[0]),
        grid=(columns // BLOCK,),
        in_specs=[block, block, block, pl.BlockSpec(coefs.shape, lambda i: (0, 0, 0, 0))],
        out_specs=block,
        out_shape=jax.ShapeDtypeStruct(vectors.shape, jnp.float32),
        scratch_shapes=[pltpu.VMEM((3 * rows, sites, BLOCK), jnp.float32)] * 2,
        compiler_params=pltpu.CompilerParams(vmem_limit_bytes=40 * MIB),
        name="slices",
    )(vectors, low, high, coefs)


def eliminate(mat_ref, inv_ref):
    size = mat_ref.shape[0]
    step = 8
    wide = (step, 2 * size)
    lanes = lax.broadcasted_iota(jnp.int32, (step, size), 1)
    subs = lax.broadcasted_iota(jnp.int32, wide, 0)
    inv_ref[...] = identity(size)
    for first in range(0, size, step):
        last = first + step
        both = jnp.concatenate([mat_ref[first:last], inv_ref[first:last]], 1)
        columns = [jnp.broadcast_to(both[:, first + k:first + k + 1], (step, size)) for k in range(step)]
        entry = [[jnp.broadcast_to(columns[k][i:i + 1], (step, size)) for k in range(i + 1)] for i in range(step)]
        rows = [jnp.broadcast_to(both[i:i + 1], wide) for i in range(step)]
        result = jnp.zeros(wide, jnp.float32)
        for k in range(step):
            root = lax.rsqrt(entry[k][k])
            done = rows[k] * jnp.concatenate([root, root], 1)
            result = jnp.where(subs == k, done, result)
            lower = {i: entry[i][k] * root for i in range(k + 1, step)}
            for i in range(k + 1, step):
                for j in range(k + 1, i + 1):
                    entry[i][j] = entry[i][j] - lower[i] * lower[j]
                rows[i] = rows[i] - jnp.concatenate([lower[i], lower[i]], 1) * done
        inv_ref[first:last] = result[:, size:]
        if last < size:
            below = jnp.where(lanes >= last, result[:, :size], 0.0)
            change = dot(below, result, (0, 0))
            mat_ref[last:] = mat_ref[last:] - change[last:, :size]
            inv_ref[last:] = inv_ref[last:] - change[last:, size:]


def identity(size):
    lanes = lax.broadcasted_iota(jnp.int32, (size, size), 1)
    subs = lax.broadcasted_iota(jnp.int32, (size, size), 0)
    return jnp.where(lanes == subs, 1.0, 0.0).astype(jnp.float32)


def block_scales(block, total):
    diag = identity(PANEL) * block
    along = lax.rsqrt(jnp.sum(diag, axis=0, keepdims=True) / total + tiny)
    down = lax.rsqrt(jnp.sum(diag, axis=1, keepdims=True) / total + tiny)
    return along, down


def products_block(sums_ref, index):
    each = sums_ref.shape[0] // 4
    return sums_ref[index * each:(index + 1) * each, :SMALL].reshape(PANEL, PANEL)


def first_kernel(total, sums_ref, rest_ref, inv_ref, cross_ref, mat_ref):
    block = products_block(sums_ref, 0)
    along0, down0 = block_scales(block, total)
    mat_ref[...] = block * down0 * along0 / total
    eliminate(mat_ref, inv_ref)
    block = products_block(sums_ref, 2)
    along1, down1 = block_scales(block, total)
    cross = dot(inv_ref[...], products_block(sums_ref, 1) * down0 * along1 / total, (1, 0))
    cross_ref[...] = cross
    rest_ref[...] = block * down1 * along1 / total - dot(cross, cross, (0, 0))


def second_kernel(total, sums_ref, rest_ref, inv0_ref, cross_ref, out_ref, mat_ref, inv_ref):
    mat_ref[...] = rest_ref[...]
    eliminate(mat_ref, inv_ref)
    along0, _ = block_scales(products_block(sums_ref, 0), total)
    along1, _ = block_scales(products_block(sums_ref, 2), total)
    inv0 = inv0_ref[...]
    inv1 = inv_ref[...]
    mixed = -dot(dot(inv1, cross_ref[...], (1, 1)), inv0, (1, 0))
    out_ref[0:PANEL, 0:PANEL] = inv0 * along0
    out_ref[0:PANEL, PANEL:] = jnp.zeros((PANEL, PANEL), jnp.float32)
    out_ref[PANEL:, 0:PANEL] = mixed * along0
    out_ref[PANEL:, PANEL:] = inv1 * along1


def call(kernel, name, outs, scratch, *args):
    square = pltpu.VMEM((PANEL, PANEL), jnp.float32)
    shapes = [jax.ShapeDtypeStruct((k * PANEL, k * PANEL), jnp.float32) for k in outs]
    return pl.pallas_call(
        kernel,
        out_shape=shapes,
        scratch_shapes=[square] * scratch,
        compiler_params=pltpu.CompilerParams(vmem_limit_bytes=16 * MIB),
        cost_estimate=pl.CostEstimate(flops=2 * 10**9, bytes_accessed=10**6, transcendentals=0),
        name=name,
    )(*args)


def first_half(sums, total):
    return call(functools.partial(first_kernel, total), "factor_a", [1, 1, 1], 1, sums)


def second_half(sums, rest, inv0, cross, total):
    return call(functools.partial(second_kernel, total), "factor_b", [2], 2, sums, rest, inv0, cross)[0]


def finish_kernel(total, place_ref, inv_ref, sums_ref, panel0_ref, panel1_ref, matrix_ref,
                  out_ref, growth_ref, weights_ref, factors_ref):
    count = out_ref.shape[3] // BLOCK
    place = place_ref[0]
    holder = place < 2
    wide = (1, count * BLOCK)

    @pl.when(pl.program_id(0) == 0)
    def _():
        each = sums_ref.shape[0] // count
        inverse = inv_ref[...]
        sums = [sums_ref[each * i:each * (i + 1), SMALL:].reshape(2 * PANEL, BLOCK) for i in range(count)]
        part = dot(inverse, jnp.concatenate(sums, 1), (1, 0)) / total
        subs = lax.broadcasted_iota(jnp.int32, part.shape, 0)
        lanes = lax.broadcasted_iota(jnp.int32, part.shape, 1)
        chosen = jnp.where(subs == lanes + place * PANEL, -1.0, 0.0)
        part = jnp.where(jnp.logical_and(lanes < PANEL, holder), chosen, part)
        weights_ref[...] = dot(inverse, part, (0, 0))
        place4 = 3 * sums_ref.shape[0] // 4
        squares = jnp.concatenate([sums_ref[place4, i:i + 1] for i in range(count)], 1)
        scale = jnp.sqrt(squares / total + tiny)
        growth_ref[...] = jnp.log(scale)
        in_panel = jnp.logical_and(lax.broadcasted_iota(jnp.int32, wide, 1) < PANEL, holder)
        factors_ref[0:1] = jnp.where(in_panel, 0.0, 1.0)
        factors_ref[1:2] = jnp.where(in_panel, 1.0, 1.0 / scale)

    panels = jnp.concatenate([panel0_ref[...], panel1_ref[...]], 1)
    taken = dot(panels, weights_ref[...], (1, 0))
    rows = taken.shape[0]
    block = matrix_ref[...].reshape(rows, -1)
    out_ref[...] = ((block * factors_ref[0:1] - taken) * factors_ref[1:2]).reshape(out_ref.shape)


def finish(col_index, inverse, sums, panel0, panel1, matrix, total):
    _, rows, sites, columns = matrix.shape
    steps = 2 if rows % 2 == 0 else 1
    block = pl.BlockSpec((1, rows // steps, sites, columns), lambda i: (i // steps, i % steps, 0, 0))
    fixed = lambda array: pl.BlockSpec(array.shape, lambda i: (0,) * array.ndim)
    panel = pl.BlockSpec((rows // steps * sites, PANEL), lambda i: (i, 0))
    return pl.pallas_call(
        functools.partial(finish_kernel, total),
        grid=(2 * steps,),
        in_specs=[
            pl.BlockSpec(memory_space=pltpu.SMEM),
            fixed(inverse),
            fixed(sums),
            panel,
            panel,
            block,
        ],
        out_specs=[block, pl.BlockSpec((1, columns), lambda i: (0, 0))],
        out_shape=[
            jax.ShapeDtypeStruct((2, rows, sites, columns), jnp.float32),
            jax.ShapeDtypeStruct((1, columns), jnp.float32),
        ],
        scratch_shapes=[
            pltpu.VMEM((2 * PANEL, columns), jnp.float32),
            pltpu.VMEM((8, columns), jnp.float32),
        ],
        compiler_params=pltpu.CompilerParams(vmem_limit_bytes=40 * MIB),
        name="finish",
    )(col_index.reshape(1), inverse, sums, panel0, panel1, matrix)


def on_device(vectors, potential):
    depth = potential.shape[0]
    _, rows, sites, columns = vectors.shape
    row_count = lax.axis_size("row")
    row_index = lax.axis_index("row")
    col_index = lax.axis_index("col")
    total = 2 * rows * sites * row_count

    col_count = lax.axis_size("col")

    def neighbours(block, cols):
        ahead = [(i * col_count + c, (i + 1) % row_count * col_count + c) for i in range(row_count) for c in cols]
        back = [(target, source) for source, target in ahead]
        return lax.ppermute(block, ("row", "col"), ahead), lax.ppermute(block, ("row", "col"), back)

    site_rows = (row_index * rows - depth + 1 + jnp.arange(rows + 2 * depth - 2)) % potential.shape[1]
    coefs = energy - site_values(jnp.take(potential, site_rows, axis=1))
    coefs = jnp.broadcast_to(coefs[..., None], coefs.shape + (BLOCK,))

    panel = vectors[..., :PANEL]
    panel = stencil(panel, *neighbours(panel, [0, 1]), coefs).reshape(-1, PANEL)
    held = jnp.where(col_index < 2, panel, 0.0)
    stages = [
        [(0, 9), (1, 8)],
        [(0, 4), (8, 12), (1, 13), (9, 5)],
        [(1, 3), (13, 15), (5, 7), (9, 11), (4, 2), (0, 14), (8, 6), (12, 10)],
    ]
    for pairs in stages:
        held = held + lax.ppermute(held, "col", pairs)
    pairs = [(4, 3), (2, 1), (0, 15), (14, 13), (12, 11), (10, 9), (8, 7), (6, 5)]
    other = lax.ppermute(held, "col", pairs + [(b, a) for a, b in pairs])
    has_first = functools.reduce(jnp.logical_or, [col_index == c for c in (0, 2, 4, 5, 7, 9, 11, 14)])
    panel0 = jnp.where(has_first, held, other)
    panel1 = jnp.where(has_first, other, held)

    blocks = stencil(vectors, *neighbours(vectors, range(col_count)), coefs)
    matrix = blocks.reshape(-1, columns)
    panels = jnp.concatenate([panel0, panel1], 1)
    coeffs = dot(panels, matrix, (0, 0))
    products = dot(panels, panels, (0, 0))
    squares = jnp.sum(matrix * matrix, 0).reshape(-1, BLOCK)
    small = jnp.concatenate([
        products[:PANEL, :PANEL],
        products[:PANEL, PANEL:],
        products[PANEL:, PANEL:],
        jnp.pad(squares, ((0, PANEL - squares.shape[0]), (0, 0))),
    ], 0)
    large = jnp.moveaxis(coeffs.reshape(2 * PANEL, -1, BLOCK), 1, 0)

    sums = jnp.concatenate([small.reshape(row_count, -1, BLOCK), large.reshape(row_count, -1, BLOCK)], 1)
    share = jnp.sum(lax.all_to_all(sums, "row", 0, 0), 0)
    sums = lax.all_to_all(jnp.broadcast_to(share, (row_count,) + share.shape), "row", 0, 0)
    inverse = second_half(sums, *first_half(sums, total), total)
    result, growth = finish(col_index, inverse, sums, panel0, panel1, blocks, total)
    return (result, growth.reshape(-1))


def solution(mesh):
    return jax.shard_map(
        on_device,
        mesh=mesh,
        in_specs=(P(None, "row", None, "col"), P()),
        out_specs=(P(None, "row", None, "col"), P("col")),
        check_vma=False,
    )
```

```python
import functools

import jax
import jax.numpy as jnp
from jax import lax
from jax.experimental import pallas as pl
from jax.experimental.pallas import tpu as pltpu
from jax.sharding import PartitionSpec as P

PANEL = 128
LEVELS = 4096
BLOCK = 128
SMALL = 16

energy = 0.25
disorder = 16.5
tiny = 1e-06
highest = lax.Precision.HIGHEST
MIB = 2**20


def site_values(codes):
    return disorder * ((codes.astype(jnp.float32) + 0.5) / LEVELS - 0.5)


def dot(left, right, contract):
    return lax.dot_general(
        left, right, ((contract[:1], contract[1:]), ((), ())),
        precision=highest, preferred_element_type=jnp.float32,
    )


def stencil_kernel(depth, vec_ref, low_ref, high_ref, coef_ref, out_ref, a_ref, b_ref):
    rows = vec_ref.shape[1]
    for i in range(rows):
        a_ref[i] = low_ref[0, i]
        a_ref[rows + i] = vec_ref[0, i]
        a_ref[2 * rows + i] = high_ref[0, i]
        b_ref[i] = low_ref[1, i]
        b_ref[rows + i] = vec_ref[1, i]
        b_ref[2 * rows + i] = high_ref[1, i]
    current, previous = a_ref, b_ref
    sites = vec_ref.shape[2]
    for step in range(depth):
        reach = depth - 1 - step

        def one_row(i, _, current=current, previous=previous, step=step):
            center = current[i]
            beside = current[i + 1] + current[i - 1]
            beside = beside + pltpu.roll(center, 1, 0) + pltpu.roll(center, sites - 1, 0)
            previous[i] = coef_ref[step, i - rows + depth - 1] * center - beside - previous[i]
            return 0

        lax.fori_loop(rows - reach, 2 * rows + reach, one_row, 0)
        current, previous = previous, current
    for i in range(rows):
        out_ref[0, i] = current[rows + i]
        out_ref[1, i] = previous[rows + i]


def stencil(vectors, low, high, coefs):
    _, rows, sites, columns = vectors.shape
    block = pl.BlockSpec((2, rows, sites, BLOCK), lambda i: (0, 0, 0, i))
    return pl.pallas_call(
        functools.partial(stencil_kernel, coefs.shape[0]),
        grid=(columns // BLOCK,),
        in_specs=[block, block, block, pl.BlockSpec(coefs.shape, lambda i: (0, 0, 0, 0))],
        out_specs=block,
        out_shape=jax.ShapeDtypeStruct(vectors.shape, jnp.float32),
        scratch_shapes=[pltpu.VMEM((3 * rows, sites, BLOCK), jnp.float32)] * 2,
        compiler_params=pltpu.CompilerParams(vmem_limit_bytes=40 * MIB),
        name="slices",
    )(vectors, low, high, coefs)


def eliminate(block):
    size = block.shape[0]
    step = 8
    wide = (step, 2 * size)
    subs = lax.broadcasted_iota(jnp.int32, wide, 0)
    both = jnp.concatenate([block, identity(size)], 1)
    parts = [both[first:first + step] for first in range(0, size, step)]
    spread = lambda value: jnp.broadcast_to(value, (step, size))
    twice = lambda value: jnp.concatenate([value, value], 1)
    inverse = []
    for index, part in enumerate(parts):
        first = index * step
        more = index + 1 < len(parts)
        columns = [spread(part[:, first + k:first + k + 1]) for k in range(step)]
        entry = [[spread(columns[k][i:i + 1]) for k in range(i + 1)] for i in range(step)]
        rows = [jnp.broadcast_to(part[i:i + 1], wide) for i in range(step)]
        if more:
            after = parts[index + 1]
            beside = [spread(after[:, first + k:first + k + 1]) for k in range(step)]
        result = jnp.zeros(wide, jnp.float32)
        for k in range(step):
            root = lax.rsqrt(entry[k][k])
            done = rows[k] * twice(root)
            result = jnp.where(subs == k, done, result)
            lower = {i: entry[i][k] * root for i in range(k + 1, step)}
            for i in range(k + 1, step):
                for j in range(k + 1, i + 1):
                    entry[i][j] = entry[i][j] - lower[i] * lower[j]
                rows[i] = rows[i] - twice(lower[i]) * done
            if more:
                factor = beside[k] * root
                for j in range(k + 1, step):
                    beside[j] = beside[j] - factor * lower[j]
                after = after - twice(factor) * done
        inverse.append(result[:, size:])
        if more:
            parts[index + 1] = after
        if index + 2 < len(parts):
            change = dot(result[:, :size], result, (0, 0))
            for later in range(index + 2, len(parts)):
                parts[later] = parts[later] - change[later * step:(later + 1) * step]
    return jnp.concatenate(inverse, 0)


def identity(size):
    lanes = lax.broadcasted_iota(jnp.int32, (size, size), 1)
    subs = lax.broadcasted_iota(jnp.int32, (size, size), 0)
    return jnp.where(lanes == subs, 1.0, 0.0).astype(jnp.float32)


def block_scales(block, total):
    diag = identity(PANEL) * block
    along = lax.rsqrt(jnp.sum(diag, axis=0, keepdims=True) / total + tiny)
    down = lax.rsqrt(jnp.sum(diag, axis=1, keepdims=True) / total + tiny)
    return along, down


def products_block(sums_ref, index):
    each = sums_ref.shape[0] // 4
    return sums_ref[index * each:(index + 1) * each, :SMALL].reshape(PANEL, PANEL)


def first_kernel(total, sums_ref, rest_ref, inv_ref, cross_ref):
    block = products_block(sums_ref, 0)
    along0, down0 = block_scales(block, total)
    inverse = eliminate(block * down0 * along0 / total)
    inv_ref[...] = inverse
    block = products_block(sums_ref, 2)
    along1, down1 = block_scales(block, total)
    cross = dot(inverse, products_block(sums_ref, 1) * down0 * along1 / total, (1, 0))
    cross_ref[...] = cross
    rest_ref[...] = block * down1 * along1 / total - dot(cross, cross, (0, 0))


def second_kernel(total, sums_ref, rest_ref, inv0_ref, cross_ref, out_ref):
    inv1 = eliminate(rest_ref[...])
    along0, _ = block_scales(products_block(sums_ref, 0), total)
    along1, _ = block_scales(products_block(sums_ref, 2), total)
    inv0 = inv0_ref[...]
    mixed = -dot(dot(inv1, cross_ref[...], (1, 1)), inv0, (1, 0))
    out_ref[0:PANEL, 0:PANEL] = inv0 * along0
    out_ref[0:PANEL, PANEL:] = jnp.zeros((PANEL, PANEL), jnp.float32)
    out_ref[PANEL:, 0:PANEL] = mixed * along0
    out_ref[PANEL:, PANEL:] = inv1 * along1


def call(kernel, name, outs, *args):
    shapes = [jax.ShapeDtypeStruct((k * PANEL, k * PANEL), jnp.float32) for k in outs]
    return pl.pallas_call(
        kernel,
        out_shape=shapes,
        compiler_params=pltpu.CompilerParams(vmem_limit_bytes=16 * MIB),
        name=name,
    )(*args)


def first_half(sums, total):
    return call(functools.partial(first_kernel, total), "factor_a", [1, 1, 1], sums)


def second_half(sums, rest, inv0, cross, total):
    return call(functools.partial(second_kernel, total), "factor_b", [2], sums, rest, inv0, cross)[0]


def sums_kernel(place_ref, held_ref, other_ref, matrix_ref, out_ref):
    shares = out_ref.shape[0]
    each = shares // 4
    ordered = place_ref[1] == 1
    held = held_ref[...]
    other = other_ref[...]
    panels = jnp.concatenate([jnp.where(ordered, held, other), jnp.where(ordered, other, held)], 1)
    matrix = matrix_ref[...].reshape(panels.shape[0], -1)
    products = dot(panels, jnp.concatenate([panels, matrix], 1), (0, 0))
    blocks = [products[:PANEL, :PANEL], products[:PANEL, PANEL:2 * PANEL], products[PANEL:, PANEL:2 * PANEL]]
    for i, block in enumerate(blocks):
        out_ref[i * each:(i + 1) * each, :SMALL] = block.reshape(each, SMALL, BLOCK)
    squares = jnp.sum(matrix * matrix, 0, keepdims=True)
    count = matrix.shape[1] // BLOCK
    out_ref[3 * each:, :SMALL] = jnp.zeros((shares - 3 * each, SMALL, BLOCK), jnp.float32)
    for i in range(count):
        out_ref[3 * each, i:i + 1] = squares[:, i * BLOCK:(i + 1) * BLOCK]
        block = products[:, 2 * PANEL + i * BLOCK:2 * PANEL + (i + 1) * BLOCK]
        out_ref[i * shares // count:(i + 1) * shares // count, SMALL:] = block.reshape(shares // count, -1, BLOCK)


def shared_sums(place, held, other, matrix, shares):
    columns = matrix.shape[3]
    depth = SMALL + 2 * PANEL * (columns // BLOCK) // shares
    vmem = pl.BlockSpec(memory_space=pltpu.VMEM)
    return pl.pallas_call(
        sums_kernel,
        in_specs=[pl.BlockSpec(memory_space=pltpu.SMEM), vmem, vmem, vmem],
        out_specs=vmem,
        out_shape=jax.ShapeDtypeStruct((shares, depth, BLOCK), jnp.float32),
        compiler_params=pltpu.CompilerParams(vmem_limit_bytes=48 * MIB),
        name="shared_sums",
    )(place, held, other, matrix)


def finish_kernel(total, place_ref, inv_ref, sums_ref, held_ref, other_ref, matrix_ref,
                  out_ref, growth_ref, weights_ref, factors_ref):
    count = out_ref.shape[3] // BLOCK
    place = place_ref[0]
    holder = place < 2
    wide = (1, count * BLOCK)

    @pl.when(pl.program_id(0) == 0)
    def _():
        each = sums_ref.shape[0] // count
        inverse = inv_ref[...]
        sums = [sums_ref[each * i:each * (i + 1), SMALL:].reshape(2 * PANEL, BLOCK) for i in range(count)]
        part = dot(inverse, jnp.concatenate(sums, 1), (1, 0)) / total
        subs = lax.broadcasted_iota(jnp.int32, part.shape, 0)
        lanes = lax.broadcasted_iota(jnp.int32, part.shape, 1)
        chosen = jnp.where(subs == lanes + place * PANEL, -1.0, 0.0)
        part = jnp.where(jnp.logical_and(lanes < PANEL, holder), chosen, part)
        weights = dot(inverse, part, (0, 0))
        ordered = place_ref[1] == 1
        weights_ref[:PANEL] = jnp.where(ordered, weights[:PANEL], weights[PANEL:])
        weights_ref[PANEL:] = jnp.where(ordered, weights[PANEL:], weights[:PANEL])
        place4 = 3 * sums_ref.shape[0] // 4
        squares = jnp.concatenate([sums_ref[place4, i:i + 1] for i in range(count)], 1)
        scale = jnp.sqrt(squares / total + tiny)
        growth_ref[...] = jnp.log(scale)
        in_panel = jnp.logical_and(lax.broadcasted_iota(jnp.int32, wide, 1) < PANEL, holder)
        factors_ref[0:1] = jnp.where(in_panel, 0.0, 1.0)
        factors_ref[1:2] = jnp.where(in_panel, 1.0, 1.0 / scale)

    panels = jnp.concatenate([held_ref[...], other_ref[...]], 1)
    taken = dot(panels, weights_ref[...], (1, 0))
    rows = taken.shape[0]
    block = matrix_ref[...].reshape(rows, -1)
    out_ref[...] = ((block * factors_ref[0:1] - taken) * factors_ref[1:2]).reshape(out_ref.shape)


def finish(place, inverse, sums, held, other, matrix, total):
    _, rows, sites, columns = matrix.shape
    steps = 2 if rows % 2 == 0 else 1
    block = pl.BlockSpec((1, rows // steps, sites, columns), lambda i: (i // steps, i % steps, 0, 0))
    fixed = lambda array: pl.BlockSpec(array.shape, lambda i: (0,) * array.ndim)
    panel = pl.BlockSpec((rows // steps * sites, PANEL), lambda i: (i, 0))
    return pl.pallas_call(
        functools.partial(finish_kernel, total),
        grid=(2 * steps,),
        in_specs=[
            pl.BlockSpec(memory_space=pltpu.SMEM),
            fixed(inverse),
            fixed(sums),
            panel,
            panel,
            block,
        ],
        out_specs=[block, pl.BlockSpec((1, columns), lambda i: (0, 0))],
        out_shape=[
            jax.ShapeDtypeStruct((2, rows, sites, columns), jnp.float32),
            jax.ShapeDtypeStruct((1, columns), jnp.float32),
        ],
        scratch_shapes=[
            pltpu.VMEM((2 * PANEL, columns), jnp.float32),
            pltpu.VMEM((8, columns), jnp.float32),
        ],
        compiler_params=pltpu.CompilerParams(vmem_limit_bytes=40 * MIB),
        name="finish",
    )(place, inverse, sums, held, other, matrix)


def on_device(vectors, potential):
    depth = potential.shape[0]
    _, rows, sites, columns = vectors.shape
    row_count = lax.axis_size("row")
    row_index = lax.axis_index("row")
    col_index = lax.axis_index("col")
    total = 2 * rows * sites * row_count

    col_count = lax.axis_size("col")

    def neighbours(block, cols):
        ahead = [(i * col_count + c, (i + 1) % row_count * col_count + c) for i in range(row_count) for c in cols]
        back = [(target, source) for source, target in ahead]
        return lax.ppermute(block, ("row", "col"), ahead), lax.ppermute(block, ("row", "col"), back)

    site_rows = (row_index * rows - depth + 1 + jnp.arange(rows + 2 * depth - 2)) % potential.shape[1]
    coefs = energy - site_values(jnp.take(potential, site_rows, axis=1))
    coefs = jnp.broadcast_to(coefs[..., None], coefs.shape + (BLOCK,))

    panel = vectors[..., :PANEL]
    panel = stencil(panel, *neighbours(panel, [0, 1]), coefs).reshape(-1, PANEL)
    held = jnp.where(col_index < 2, panel, 0.0)
    stages = [
        [(0, 9), (1, 8)],
        [(0, 4), (8, 12), (1, 13), (9, 5)],
        [(1, 3), (13, 15), (5, 7), (9, 11), (4, 2), (0, 14), (8, 6), (12, 10)],
    ]
    for pairs in stages:
        held = held + lax.ppermute(held, "col", pairs)
    pairs = [(4, 3), (2, 1), (0, 15), (14, 13), (12, 11), (10, 9), (8, 7), (6, 5)]
    other = lax.ppermute(held, "col", pairs + [(b, a) for a, b in pairs])
    has_first = functools.reduce(jnp.logical_or, [col_index == c for c in (0, 2, 4, 5, 7, 9, 11, 14)])
    place = jnp.stack([col_index, has_first.astype(jnp.int32)])

    blocks = stencil(vectors, *neighbours(vectors, range(col_count)), coefs)
    sums = lax.all_to_all(shared_sums(place, held, other, blocks, row_count), "row", 0, 0)
    share = jnp.sum(sums, 0)
    sums = lax.all_to_all(jnp.broadcast_to(share, (row_count,) + share.shape), "row", 0, 0)
    inverse = second_half(sums, *first_half(sums, total), total)
    result, growth = finish(place, inverse, sums, held, other, blocks, total)
    return (result, growth.reshape(-1))


def solution(mesh):
    return jax.shard_map(
        on_device,
        mesh=mesh,
        in_specs=(P(None, "row", None, "col"), P()),
        out_specs=(P(None, "row", None, "col"), P("col")),
        check_vma=False,
    )
```

```python
import functools

import jax
import jax.numpy as jnp
from jax import lax
from jax.experimental import pallas as pl
from jax.experimental.pallas import tpu as pltpu
from jax.sharding import PartitionSpec as P

PANEL = 128
LEVELS = 4096
BLOCK = 128
SMALL = 16

energy = 0.25
disorder = 16.5
tiny = 1e-06
highest = lax.Precision.HIGHEST
MIB = 2**20


def site_values(codes):
    return disorder * ((codes.astype(jnp.float32) + 0.5) / LEVELS - 0.5)


def dot(left, right, contract):
    return lax.dot_general(
        left, right, ((contract[:1], contract[1:]), ((), ())),
        precision=highest, preferred_element_type=jnp.float32,
    )


def stencil_kernel(depth, vec_ref, low_ref, high_ref, coef_ref, out_ref, a_ref, b_ref):
    rows = vec_ref.shape[1]
    for i in range(rows):
        a_ref[i] = low_ref[0, i]
        a_ref[rows + i] = vec_ref[0, i]
        a_ref[2 * rows + i] = high_ref[0, i]
        b_ref[i] = low_ref[1, i]
        b_ref[rows + i] = vec_ref[1, i]
        b_ref[2 * rows + i] = high_ref[1, i]
    current, previous = a_ref, b_ref
    sites = vec_ref.shape[2]
    for step in range(depth):
        reach = depth - 1 - step

        def one_row(i, _, current=current, previous=previous, step=step):
            center = current[i]
            beside = current[i + 1] + current[i - 1]
            beside = beside + pltpu.roll(center, 1, 0) + pltpu.roll(center, sites - 1, 0)
            previous[i] = coef_ref[step, i - rows + depth - 1] * center - beside - previous[i]
            return 0

        lax.fori_loop(rows - reach, 2 * rows + reach, one_row, 0)
        current, previous = previous, current
    for i in range(rows):
        out_ref[0, i] = current[rows + i]
        out_ref[1, i] = previous[rows + i]


def stencil(vectors, low, high, coefs):
    _, rows, sites, columns = vectors.shape
    block = pl.BlockSpec((2, rows, sites, BLOCK), lambda i: (0, 0, 0, i))
    return pl.pallas_call(
        functools.partial(stencil_kernel, coefs.shape[0]),
        grid=(columns // BLOCK,),
        in_specs=[block, block, block, pl.BlockSpec(coefs.shape, lambda i: (0, 0, 0, 0))],
        out_specs=block,
        out_shape=jax.ShapeDtypeStruct(vectors.shape, jnp.float32),
        scratch_shapes=[pltpu.VMEM((3 * rows, sites, BLOCK), jnp.float32)] * 2,
        compiler_params=pltpu.CompilerParams(vmem_limit_bytes=16 * MIB),
        name="slices",
    )(vectors, low, high, coefs)


def eliminate(block):
    size = block.shape[0]
    step = 8
    wide = (step, 2 * size)
    subs = lax.broadcasted_iota(jnp.int32, wide, 0)
    both = jnp.concatenate([block, identity(size)], 1)
    parts = [both[first:first + step] for first in range(0, size, step)]
    spread = lambda value: jnp.broadcast_to(value, (step, size))
    twice = lambda value: jnp.concatenate([value, value], 1)
    inverse = []
    for index, part in enumerate(parts):
        first = index * step
        more = index + 1 < len(parts)
        columns = [spread(part[:, first + k:first + k + 1]) for k in range(step)]
        entry = [[spread(columns[k][i:i + 1]) for k in range(i + 1)] for i in range(step)]
        rows = [jnp.broadcast_to(part[i:i + 1], wide) for i in range(step)]
        if more:
            after = parts[index + 1]
            beside = [spread(after[:, first + k:first + k + 1]) for k in range(step)]
        result = jnp.zeros(wide, jnp.float32)
        for k in range(step):
            root = lax.rsqrt(entry[k][k])
            done = rows[k] * twice(root)
            result = jnp.where(subs == k, done, result)
            lower = {i: entry[i][k] * root for i in range(k + 1, step)}
            for i in range(k + 1, step):
                for j in range(k + 1, i + 1):
                    entry[i][j] = entry[i][j] - lower[i] * lower[j]
                rows[i] = rows[i] - twice(lower[i]) * done
            if more:
                factor = beside[k] * root
                for j in range(k + 1, step):
                    beside[j] = beside[j] - factor * lower[j]
                after = after - twice(factor) * done
        inverse.append(result[:, size:])
        if more:
            parts[index + 1] = after
        if index + 2 < len(parts):
            change = dot(result[:, :size], result, (0, 0))
            for later in range(index + 2, len(parts)):
                parts[later] = parts[later] - change[later * step:(later + 1) * step]
    return jnp.concatenate(inverse, 0)


def identity(size):
    lanes = lax.broadcasted_iota(jnp.int32, (size, size), 1)
    subs = lax.broadcasted_iota(jnp.int32, (size, size), 0)
    return jnp.where(lanes == subs, 1.0, 0.0).astype(jnp.float32)


def block_scales(block, total):
    diag = identity(PANEL) * block
    along = lax.rsqrt(jnp.sum(diag, axis=0, keepdims=True) / total + tiny)
    down = lax.rsqrt(jnp.sum(diag, axis=1, keepdims=True) / total + tiny)
    return along, down


def products_block(sums_ref, index):
    each = sums_ref.shape[0] // 4
    return sums_ref[index * each:(index + 1) * each, :SMALL].reshape(PANEL, PANEL)


def inverse_factor(total, sums_ref):
    block = products_block(sums_ref, 0)
    along0, down0 = block_scales(block, total)
    inv0 = eliminate(block * down0 * along0 / total)
    block = products_block(sums_ref, 2)
    along1, down1 = block_scales(block, total)
    cross = dot(inv0, products_block(sums_ref, 1) * down0 * along1 / total, (1, 0))
    inv1 = eliminate(block * down1 * along1 / total - dot(cross, cross, (0, 0)))
    mixed = -dot(dot(inv1, cross, (1, 1)), inv0, (1, 0))
    above = jnp.concatenate([inv0 * along0, jnp.zeros((PANEL, PANEL), jnp.float32)], 1)
    below = jnp.concatenate([mixed * along0, inv1 * along1], 1)
    return jnp.concatenate([above, below], 0)


def sums_kernel(place_ref, held_ref, other_ref, matrix_ref, out_ref):
    shares = out_ref.shape[0]
    each = shares // 4
    ordered = place_ref[1] == 1
    held = held_ref[...]
    other = other_ref[...]
    panels = jnp.concatenate([jnp.where(ordered, held, other), jnp.where(ordered, other, held)], 1)
    matrix = matrix_ref[...].reshape(panels.shape[0], -1)
    products = dot(panels, jnp.concatenate([panels, matrix], 1), (0, 0))
    blocks = [products[:PANEL, :PANEL], products[:PANEL, PANEL:2 * PANEL], products[PANEL:, PANEL:2 * PANEL]]
    for i, block in enumerate(blocks):
        out_ref[i * each:(i + 1) * each, :SMALL] = block.reshape(each, SMALL, BLOCK)
    squares = jnp.sum(matrix * matrix, 0, keepdims=True)
    count = matrix.shape[1] // BLOCK
    out_ref[3 * each:, :SMALL] = jnp.zeros((shares - 3 * each, SMALL, BLOCK), jnp.float32)
    for i in range(count):
        out_ref[3 * each, i:i + 1] = squares[:, i * BLOCK:(i + 1) * BLOCK]
        block = products[:, 2 * PANEL + i * BLOCK:2 * PANEL + (i + 1) * BLOCK]
        out_ref[i * shares // count:(i + 1) * shares // count, SMALL:] = block.reshape(shares // count, -1, BLOCK)


def shared_sums(place, held, other, matrix, shares):
    columns = matrix.shape[3]
    depth = SMALL + 2 * PANEL * (columns // BLOCK) // shares
    vmem = pl.BlockSpec(memory_space=pltpu.VMEM)
    return pl.pallas_call(
        sums_kernel,
        in_specs=[pl.BlockSpec(memory_space=pltpu.SMEM), vmem, vmem, vmem],
        out_specs=vmem,
        out_shape=jax.ShapeDtypeStruct((shares, depth, BLOCK), jnp.float32),
        compiler_params=pltpu.CompilerParams(vmem_limit_bytes=24 * MIB),
        name="shared_sums",
    )(place, held, other, matrix)


def finish_kernel(total, place_ref, sums_ref, held_ref, other_ref, matrix_ref,
                  out_ref, growth_ref, weights_ref, factors_ref):
    count = out_ref.shape[3] // BLOCK
    place = place_ref[0]
    holder = place < 2
    wide = (1, count * BLOCK)

    @pl.when(pl.program_id(0) == 0)
    def _():
        each = sums_ref.shape[0] // count
        inverse = inverse_factor(total, sums_ref)
        sums = [sums_ref[each * i:each * (i + 1), SMALL:].reshape(2 * PANEL, BLOCK) for i in range(count)]
        part = dot(inverse, jnp.concatenate(sums, 1), (1, 0)) / total
        subs = lax.broadcasted_iota(jnp.int32, part.shape, 0)
        lanes = lax.broadcasted_iota(jnp.int32, part.shape, 1)
        chosen = jnp.where(subs == lanes + place * PANEL, -1.0, 0.0)
        part = jnp.where(jnp.logical_and(lanes < PANEL, holder), chosen, part)
        weights = dot(inverse, part, (0, 0))
        ordered = place_ref[1] == 1
        weights_ref[:PANEL] = jnp.where(ordered, weights[:PANEL], weights[PANEL:])
        weights_ref[PANEL:] = jnp.where(ordered, weights[PANEL:], weights[:PANEL])
        place4 = 3 * sums_ref.shape[0] // 4
        squares = jnp.concatenate([sums_ref[place4, i:i + 1] for i in range(count)], 1)
        scale = jnp.sqrt(squares / total + tiny)
        growth_ref[...] = jnp.log(scale)
        in_panel = jnp.logical_and(lax.broadcasted_iota(jnp.int32, wide, 1) < PANEL, holder)
        factors_ref[0:1] = jnp.where(in_panel, 0.0, 1.0)
        factors_ref[1:2] = jnp.where(in_panel, 1.0, 1.0 / scale)

    panels = jnp.concatenate([held_ref[...], other_ref[...]], 1)
    taken = dot(panels, weights_ref[...], (1, 0))
    rows = taken.shape[0]
    block = matrix_ref[...].reshape(rows, -1)
    out_ref[...] = ((block * factors_ref[0:1] - taken) * factors_ref[1:2]).reshape(out_ref.shape)


def finish(place, sums, held, other, matrix, total):
    _, rows, sites, columns = matrix.shape
    steps = 2 if rows % 2 == 0 else 1
    block = pl.BlockSpec((1, rows // steps, sites, columns), lambda i: (i // steps, i % steps, 0, 0))
    fixed = lambda array: pl.BlockSpec(array.shape, lambda i: (0,) * array.ndim)
    panel = pl.BlockSpec((rows // steps * sites, PANEL), lambda i: (i, 0))
    return pl.pallas_call(
        functools.partial(finish_kernel, total),
        grid=(2 * steps,),
        in_specs=[
            pl.BlockSpec(memory_space=pltpu.SMEM),
            fixed(sums),
            panel,
            panel,
            block,
        ],
        out_specs=[block, pl.BlockSpec((1, columns), lambda i: (0, 0))],
        out_shape=[
            jax.ShapeDtypeStruct((2, rows, sites, columns), jnp.float32),
            jax.ShapeDtypeStruct((1, columns), jnp.float32),
        ],
        scratch_shapes=[
            pltpu.VMEM((2 * PANEL, columns), jnp.float32),
            pltpu.VMEM((8, columns), jnp.float32),
        ],
        compiler_params=pltpu.CompilerParams(vmem_limit_bytes=20 * MIB),
        name="finish",
    )(place, sums, held, other, matrix)


def on_device(vectors, potential):
    depth = potential.shape[0]
    _, rows, sites, columns = vectors.shape
    row_count = lax.axis_size("row")
    row_index = lax.axis_index("row")
    col_index = lax.axis_index("col")
    total = 2 * rows * sites * row_count

    col_count = lax.axis_size("col")

    def neighbours(block, cols):
        ahead = [(i * col_count + c, (i + 1) % row_count * col_count + c) for i in range(row_count) for c in cols]
        back = [(target, source) for source, target in ahead]
        return lax.ppermute(block, ("row", "col"), ahead), lax.ppermute(block, ("row", "col"), back)

    site_rows = (row_index * rows - depth + 1 + jnp.arange(rows + 2 * depth - 2)) % potential.shape[1]
    coefs = energy - site_values(jnp.take(potential, site_rows, axis=1))
    coefs = jnp.broadcast_to(coefs[..., None], coefs.shape + (BLOCK,))

    panel = vectors[..., :PANEL]
    panel = stencil(panel, *neighbours(panel, [0, 1]), coefs).reshape(-1, PANEL)
    held = jnp.where(col_index < 2, panel, 0.0)
    stages = [
        [(0, 9), (1, 8)],
        [(0, 4), (8, 12), (1, 13), (9, 5)],
        [(1, 3), (13, 15), (5, 7), (9, 11), (4, 2), (0, 14), (8, 6), (12, 10)],
    ]
    for pairs in stages:
        held = held + lax.ppermute(held, "col", pairs)
    pairs = [(4, 3), (2, 1), (0, 15), (14, 13), (12, 11), (10, 9), (8, 7), (6, 5)]
    other = lax.ppermute(held, "col", pairs + [(b, a) for a, b in pairs])
    has_first = functools.reduce(jnp.logical_or, [col_index == c for c in (0, 2, 4, 5, 7, 9, 11, 14)])
    place = jnp.stack([col_index, has_first.astype(jnp.int32)])

    blocks = stencil(vectors, *neighbours(vectors, range(col_count)), coefs)
    sums = lax.all_to_all(shared_sums(place, held, other, blocks, row_count), "row", 0, 0)
    share = jnp.sum(sums, 0)
    sums = lax.all_to_all(jnp.broadcast_to(share, (row_count,) + share.shape), "row", 0, 0)
    result, growth = finish(place, sums, held, other, blocks, total)
    return (result, growth.reshape(-1))


def solution(mesh):
    return jax.shard_map(
        on_device,
        mesh=mesh,
        in_specs=(P(None, "row", None, "col"), P()),
        out_specs=(P(None, "row", None, "col"), P("col")),
        check_vma=False,
    )
```

```python
import functools

import jax
import jax.numpy as jnp
from jax import lax
from jax.experimental import pallas as pl
from jax.experimental.pallas import tpu as pltpu
from jax.sharding import PartitionSpec as P

PANEL = 128
LEVELS = 4096
BLOCK = 128
SMALL = 16

energy = 0.25
disorder = 16.5
tiny = 1e-06
highest = lax.Precision.HIGHEST
MIB = 2**20


def site_values(codes):
    return disorder * ((codes.astype(jnp.float32) + 0.5) / LEVELS - 0.5)


def dot(left, right, contract):
    return lax.dot_general(
        left, right, ((contract[:1], contract[1:]), ((), ())),
        precision=highest, preferred_element_type=jnp.float32,
    )


def stencil_kernel(depth, vec_ref, low_ref, high_ref, coef_ref, out_ref, a_ref, b_ref):
    rows = vec_ref.shape[1]
    for i in range(rows):
        a_ref[i] = low_ref[0, i]
        a_ref[rows + i] = vec_ref[0, i]
        a_ref[2 * rows + i] = high_ref[0, i]
        b_ref[i] = low_ref[1, i]
        b_ref[rows + i] = vec_ref[1, i]
        b_ref[2 * rows + i] = high_ref[1, i]
    current, previous = a_ref, b_ref
    sites = vec_ref.shape[2]
    for step in range(depth):
        reach = depth - 1 - step

        def one_row(i, _, current=current, previous=previous, step=step):
            center = current[i]
            beside = current[i + 1] + current[i - 1]
            beside = beside + pltpu.roll(center, 1, 0) + pltpu.roll(center, sites - 1, 0)
            along = coef_ref[step, pl.ds(i - rows + depth - 1, 1), :]
            coef = jnp.broadcast_to(along, (center.shape[1], sites)).T
            previous[i] = coef * center - beside - previous[i]
            return 0

        lax.fori_loop(rows - reach, 2 * rows + reach, one_row, 0)
        current, previous = previous, current
    for i in range(rows):
        out_ref[0, i] = current[rows + i]
        out_ref[1, i] = previous[rows + i]


def stencil(vectors, low, high, coefs):
    _, rows, sites, columns = vectors.shape
    block = pl.BlockSpec((2, rows, sites, BLOCK), lambda i: (0, 0, 0, i))
    return pl.pallas_call(
        functools.partial(stencil_kernel, coefs.shape[0]),
        grid=(columns // BLOCK,),
        in_specs=[block, block, block, pl.BlockSpec(coefs.shape, lambda i: (0, 0, 0))],
        out_specs=block,
        out_shape=jax.ShapeDtypeStruct(vectors.shape, jnp.float32),
        scratch_shapes=[pltpu.VMEM((3 * rows, sites, BLOCK), jnp.float32)] * 2,
        compiler_params=pltpu.CompilerParams(vmem_limit_bytes=40 * MIB),
        name="slices",
    )(vectors, low, high, coefs)


def eliminate(block):
    size = block.shape[0]
    step = 8
    wide = (step, 2 * size)
    subs = lax.broadcasted_iota(jnp.int32, wide, 0)
    both = jnp.concatenate([block, identity(size)], 1)
    parts = [both[first:first + step] for first in range(0, size, step)]
    spread = lambda value: jnp.broadcast_to(value, (step, size))
    twice = lambda value: jnp.concatenate([value, value], 1)
    inverse = []
    for index, part in enumerate(parts):
        first = index * step
        more = index + 1 < len(parts)
        columns = [spread(part[:, first + k:first + k + 1]) for k in range(step)]
        entry = [[spread(columns[k][i:i + 1]) for k in range(i + 1)] for i in range(step)]
        rows = [jnp.broadcast_to(part[i:i + 1], wide) for i in range(step)]
        if more:
            after = parts[index + 1]
            beside = [spread(after[:, first + k:first + k + 1]) for k in range(step)]
        result = jnp.zeros(wide, jnp.float32)
        for k in range(step):
            root = lax.rsqrt(entry[k][k])
            done = rows[k] * twice(root)
            result = jnp.where(subs == k, done, result)
            lower = {i: entry[i][k] * root for i in range(k + 1, step)}
            for i in range(k + 1, step):
                for j in range(k + 1, i + 1):
                    entry[i][j] = entry[i][j] - lower[i] * lower[j]
                rows[i] = rows[i] - twice(lower[i]) * done
            if more:
                factor = beside[k] * root
                for j in range(k + 1, step):
                    beside[j] = beside[j] - factor * lower[j]
                after = after - twice(factor) * done
        inverse.append(result[:, size:])
        if more:
            parts[index + 1] = after
        if index + 2 < len(parts):
            change = dot(result[:, :size], result, (0, 0))
            for later in range(index + 2, len(parts)):
                parts[later] = parts[later] - change[later * step:(later + 1) * step]
    return jnp.concatenate(inverse, 0)


def identity(size):
    lanes = lax.broadcasted_iota(jnp.int32, (size, size), 1)
    subs = lax.broadcasted_iota(jnp.int32, (size, size), 0)
    return jnp.where(lanes == subs, 1.0, 0.0).astype(jnp.float32)


def block_scales(block, total):
    diag = identity(PANEL) * block
    along = lax.rsqrt(jnp.sum(diag, axis=0, keepdims=True) / total + tiny)
    down = lax.rsqrt(jnp.sum(diag, axis=1, keepdims=True) / total + tiny)
    return along, down


def products_block(sums_ref, index):
    each = sums_ref.shape[0] // 4
    return sums_ref[index * each:(index + 1) * each, :SMALL].reshape(PANEL, PANEL)


def first_kernel(total, sums_ref, rest_ref, inv_ref, cross_ref):
    block = products_block(sums_ref, 0)
    along0, down0 = block_scales(block, total)
    inverse = eliminate(block * down0 * along0 / total)
    inv_ref[...] = inverse
    block = products_block(sums_ref, 2)
    along1, down1 = block_scales(block, total)
    cross = dot(inverse, products_block(sums_ref, 1) * down0 * along1 / total, (1, 0))
    cross_ref[...] = cross
    rest_ref[...] = block * down1 * along1 / total - dot(cross, cross, (0, 0))


def second_kernel(total, sums_ref, rest_ref, inv0_ref, cross_ref, out_ref):
    inv1 = eliminate(rest_ref[...])
    along0, _ = block_scales(products_block(sums_ref, 0), total)
    along1, _ = block_scales(products_block(sums_ref, 2), total)
    inv0 = inv0_ref[...]
    mixed = -dot(dot(inv1, cross_ref[...], (1, 1)), inv0, (1, 0))
    out_ref[0:PANEL, 0:PANEL] = inv0 * along0
    out_ref[0:PANEL, PANEL:] = jnp.zeros((PANEL, PANEL), jnp.float32)
    out_ref[PANEL:, 0:PANEL] = mixed * along0
    out_ref[PANEL:, PANEL:] = inv1 * along1


def call(kernel, name, outs, *args):
    shapes = [jax.ShapeDtypeStruct((k * PANEL, k * PANEL), jnp.float32) for k in outs]
    return pl.pallas_call(
        kernel,
        out_shape=shapes,
        compiler_params=pltpu.CompilerParams(vmem_limit_bytes=16 * MIB),
        name=name,
    )(*args)


def first_half(sums, total):
    return call(functools.partial(first_kernel, total), "factor_a", [1, 1, 1], sums)


def second_half(sums, rest, inv0, cross, total):
    return call(functools.partial(second_kernel, total), "factor_b", [2], sums, rest, inv0, cross)[0]


def sums_kernel(place_ref, held_ref, other_ref, matrix_ref, out_ref):
    shares = out_ref.shape[0]
    each = shares // 4
    ordered = place_ref[1] == 1
    held = held_ref[...]
    other = other_ref[...]
    panels = jnp.concatenate([jnp.where(ordered, held, other), jnp.where(ordered, other, held)], 1)
    matrix = matrix_ref[...].reshape(panels.shape[0], -1)
    products = dot(panels, jnp.concatenate([panels, matrix], 1), (0, 0))
    blocks = [products[:PANEL, :PANEL], products[:PANEL, PANEL:2 * PANEL], products[PANEL:, PANEL:2 * PANEL]]
    for i, block in enumerate(blocks):
        out_ref[i * each:(i + 1) * each, :SMALL] = block.reshape(each, SMALL, BLOCK)
    squares = jnp.sum(matrix * matrix, 0, keepdims=True)
    count = matrix.shape[1] // BLOCK
    out_ref[3 * each:, :SMALL] = jnp.zeros((shares - 3 * each, SMALL, BLOCK), jnp.float32)
    for i in range(count):
        out_ref[3 * each, i:i + 1] = squares[:, i * BLOCK:(i + 1) * BLOCK]
        block = products[:, 2 * PANEL + i * BLOCK:2 * PANEL + (i + 1) * BLOCK]
        out_ref[i * shares // count:(i + 1) * shares // count, SMALL:] = block.reshape(shares // count, -1, BLOCK)


def shared_sums(place, held, other, matrix, shares):
    columns = matrix.shape[3]
    depth = SMALL + 2 * PANEL * (columns // BLOCK) // shares
    vmem = pl.BlockSpec(memory_space=pltpu.VMEM)
    return pl.pallas_call(
        sums_kernel,
        in_specs=[pl.BlockSpec(memory_space=pltpu.SMEM), vmem, vmem, vmem],
        out_specs=vmem,
        out_shape=jax.ShapeDtypeStruct((shares, depth, BLOCK), jnp.float32),
        compiler_params=pltpu.CompilerParams(vmem_limit_bytes=48 * MIB),
        name="shared_sums",
    )(place, held, other, matrix)


def finish_kernel(total, place_ref, inv_ref, sums_ref, held_ref, other_ref, matrix_ref,
                  out_ref, growth_ref, weights_ref, factors_ref):
    count = out_ref.shape[3] // BLOCK
    place = place_ref[0]
    holder = place < 2
    wide = (1, count * BLOCK)

    @pl.when(pl.program_id(0) == 0)
    def _():
        each = sums_ref.shape[0] // count
        inverse = inv_ref[...]
        sums = [sums_ref[each * i:each * (i + 1), SMALL:].reshape(2 * PANEL, BLOCK) for i in range(count)]
        part = dot(inverse, jnp.concatenate(sums, 1), (1, 0)) / total
        subs = lax.broadcasted_iota(jnp.int32, part.shape, 0)
        lanes = lax.broadcasted_iota(jnp.int32, part.shape, 1)
        chosen = jnp.where(subs == lanes + place * PANEL, -1.0, 0.0)
        part = jnp.where(jnp.logical_and(lanes < PANEL, holder), chosen, part)
        weights = dot(inverse, part, (0, 0))
        ordered = place_ref[1] == 1
        weights_ref[:PANEL] = jnp.where(ordered, weights[:PANEL], weights[PANEL:])
        weights_ref[PANEL:] = jnp.where(ordered, weights[PANEL:], weights[:PANEL])
        place4 = 3 * sums_ref.shape[0] // 4
        squares = jnp.concatenate([sums_ref[place4, i:i + 1] for i in range(count)], 1)
        scale = jnp.sqrt(squares / total + tiny)
        growth_ref[...] = jnp.log(scale)
        in_panel = jnp.logical_and(lax.broadcasted_iota(jnp.int32, wide, 1) < PANEL, holder)
        factors_ref[0:1] = jnp.where(in_panel, 0.0, 1.0)
        factors_ref[1:2] = jnp.where(in_panel, 1.0, 1.0 / scale)

    panels = jnp.concatenate([held_ref[...], other_ref[...]], 1)
    taken = dot(panels, weights_ref[...], (1, 0))
    rows = taken.shape[0]
    block = matrix_ref[...].reshape(rows, -1)
    out_ref[...] = ((block * factors_ref[0:1] - taken) * factors_ref[1:2]).reshape(out_ref.shape)


def finish(place, inverse, sums, held, other, matrix, total):
    _, rows, sites, columns = matrix.shape
    steps = 2 if rows % 2 == 0 else 1
    block = pl.BlockSpec((1, rows // steps, sites, columns), lambda i: (i // steps, i % steps, 0, 0))
    fixed = lambda array: pl.BlockSpec(array.shape, lambda i: (0,) * array.ndim)
    panel = pl.BlockSpec((rows // steps * sites, PANEL), lambda i: (i, 0))
    return pl.pallas_call(
        functools.partial(finish_kernel, total),
        grid=(2 * steps,),
        in_specs=[
            pl.BlockSpec(memory_space=pltpu.SMEM),
            fixed(inverse),
            fixed(sums),
            panel,
            panel,
            block,
        ],
        out_specs=[block, pl.BlockSpec((1, columns), lambda i: (0, 0))],
        out_shape=[
            jax.ShapeDtypeStruct((2, rows, sites, columns), jnp.float32),
            jax.ShapeDtypeStruct((1, columns), jnp.float32),
        ],
        scratch_shapes=[
            pltpu.VMEM((2 * PANEL, columns), jnp.float32),
            pltpu.VMEM((8, columns), jnp.float32),
        ],
        compiler_params=pltpu.CompilerParams(vmem_limit_bytes=40 * MIB),
        name="finish",
    )(place, inverse, sums, held, other, matrix)


def on_device(vectors, potential):
    depth = potential.shape[0]
    _, rows, sites, columns = vectors.shape
    row_count = lax.axis_size("row")
    row_index = lax.axis_index("row")
    col_index = lax.axis_index("col")
    total = 2 * rows * sites * row_count

    col_count = lax.axis_size("col")

    def neighbours(block, cols):
        ahead = [(i * col_count + c, (i + 1) % row_count * col_count + c) for i in range(row_count) for c in cols]
        back = [(target, source) for source, target in ahead]
        return lax.ppermute(block, ("row", "col"), ahead), lax.ppermute(block, ("row", "col"), back)

    site_rows = (row_index * rows - depth + 1 + jnp.arange(rows + 2 * depth - 2)) % potential.shape[1]
    coefs = energy - site_values(jnp.take(potential, site_rows, axis=1))

    panel = vectors[..., :PANEL]
    panel = stencil(panel, *neighbours(panel, [0, 1]), coefs).reshape(-1, PANEL)
    held = jnp.where(col_index < 2, panel, 0.0)
    stages = [
        [(0, 9), (1, 8)],
        [(0, 4), (8, 12), (1, 13), (9, 5)],
        [(1, 3), (13, 15), (5, 7), (9, 11), (4, 2), (0, 14), (8, 6), (12, 10)],
    ]
    for pairs in stages:
        held = held + lax.ppermute(held, "col", pairs)
    pairs = [(4, 3), (2, 1), (0, 15), (14, 13), (12, 11), (10, 9), (8, 7), (6, 5)]
    other = lax.ppermute(held, "col", pairs + [(b, a) for a, b in pairs])
    has_first = functools.reduce(jnp.logical_or, [col_index == c for c in (0, 2, 4, 5, 7, 9, 11, 14)])
    place = jnp.stack([col_index, has_first.astype(jnp.int32)])

    blocks = stencil(vectors, *neighbours(vectors, range(col_count)), coefs)
    sums = lax.all_to_all(shared_sums(place, held, other, blocks, row_count), "row", 0, 0)
    share = jnp.sum(sums, 0)
    sums = lax.all_to_all(jnp.broadcast_to(share, (row_count,) + share.shape), "row", 0, 0)
    inverse = second_half(sums, *first_half(sums, total), total)
    result, growth = finish(place, inverse, sums, held, other, blocks, total)
    return (result, growth.reshape(-1))


def solution(mesh):
    return jax.shard_map(
        on_device,
        mesh=mesh,
        in_specs=(P(None, "row", None, "col"), P()),
        out_specs=(P(None, "row", None, "col"), P("col")),
        check_vma=False,
    )
```

```python
import functools

import jax
import jax.numpy as jnp
from jax import lax
from jax.experimental import pallas as pl
from jax.experimental.pallas import tpu as pltpu
from jax.sharding import PartitionSpec as P

PANEL = 128
LEVELS = 4096
BLOCK = 128
SMALL = 16

energy = 0.25
disorder = 16.5
tiny = 1e-06
highest = lax.Precision.HIGHEST
MIB = 2**20


def site_values(codes):
    return disorder * ((codes.astype(jnp.float32) + 0.5) / LEVELS - 0.5)


def dot(left, right, contract):
    return lax.dot_general(
        left, right, ((contract[:1], contract[1:]), ((), ())),
        precision=highest, preferred_element_type=jnp.float32,
    )


def stencil_kernel(depth, vec_ref, low_ref, high_ref, coef_ref, out_ref, a_ref, b_ref):
    rows = vec_ref.shape[1]
    for i in range(rows):
        a_ref[i] = low_ref[0, i]
        a_ref[rows + i] = vec_ref[0, i]
        a_ref[2 * rows + i] = high_ref[0, i]
        b_ref[i] = low_ref[1, i]
        b_ref[rows + i] = vec_ref[1, i]
        b_ref[2 * rows + i] = high_ref[1, i]
    current, previous = a_ref, b_ref
    sites = vec_ref.shape[2]
    for step in range(depth):
        reach = depth - 1 - step

        for i in range(rows - reach, 2 * rows + reach):
            center = current[i]
            beside = current[i + 1] + current[i - 1]
            beside = beside + pltpu.roll(center, 1, 0) + pltpu.roll(center, sites - 1, 0)
            k = step * (rows + 2 * depth - 2) + i - rows + depth - 1
            coef = jnp.broadcast_to(coef_ref[:, k:k + 1], center.shape)
            previous[i] = coef * center - beside - previous[i]
        current, previous = previous, current
    for i in range(rows):
        out_ref[0, i] = current[rows + i]
        out_ref[1, i] = previous[rows + i]


def stencil(vectors, low, high, coefs, depth):
    _, rows, sites, columns = vectors.shape
    block = pl.BlockSpec((2, rows, sites, BLOCK), lambda i: (0, 0, 0, i))
    return pl.pallas_call(
        functools.partial(stencil_kernel, depth),
        grid=(columns // BLOCK,),
        in_specs=[block, block, block, pl.BlockSpec(coefs.shape, lambda i: (0, 0))],
        out_specs=block,
        out_shape=jax.ShapeDtypeStruct(vectors.shape, jnp.float32),
        scratch_shapes=[pltpu.VMEM((3 * rows, sites, BLOCK), jnp.float32)] * 2,
        compiler_params=pltpu.CompilerParams(vmem_limit_bytes=40 * MIB),
        name="slices",
    )(vectors, low, high, coefs)


def eliminate(block):
    size = block.shape[0]
    step = 8
    wide = (step, 2 * size)
    subs = lax.broadcasted_iota(jnp.int32, wide, 0)
    both = jnp.concatenate([block, identity(size)], 1)
    parts = [both[first:first + step] for first in range(0, size, step)]
    spread = lambda value: jnp.broadcast_to(value, (step, size))
    twice = lambda value: jnp.concatenate([value, value], 1)
    inverse = []
    for index, part in enumerate(parts):
        first = index * step
        more = index + 1 < len(parts)
        columns = [spread(part[:, first + k:first + k + 1]) for k in range(step)]
        entry = [[spread(columns[k][i:i + 1]) for k in range(i + 1)] for i in range(step)]
        rows = [jnp.broadcast_to(part[i:i + 1], wide) for i in range(step)]
        if more:
            after = parts[index + 1]
            beside = [spread(after[:, first + k:first + k + 1]) for k in range(step)]
        result = jnp.zeros(wide, jnp.float32)
        for k in range(step):
            root = lax.rsqrt(entry[k][k])
            done = rows[k] * twice(root)
            result = jnp.where(subs == k, done, result)
            lower = {i: entry[i][k] * root for i in range(k + 1, step)}
            for i in range(k + 1, step):
                for j in range(k + 1, i + 1):
                    entry[i][j] = entry[i][j] - lower[i] * lower[j]
                rows[i] = rows[i] - twice(lower[i]) * done
            if more:
                factor = beside[k] * root
                for j in range(k + 1, step):
                    beside[j] = beside[j] - factor * lower[j]
                after = after - twice(factor) * done
        inverse.append(result[:, size:])
        if more:
            parts[index + 1] = after
        if index + 2 < len(parts):
            change = dot(result[:, :size], result, (0, 0))
            for later in range(index + 2, len(parts)):
                parts[later] = parts[later] - change[later * step:(later + 1) * step]
    return jnp.concatenate(inverse, 0)


def identity(size):
    lanes = lax.broadcasted_iota(jnp.int32, (size, size), 1)
    subs = lax.broadcasted_iota(jnp.int32, (size, size), 0)
    return jnp.where(lanes == subs, 1.0, 0.0).astype(jnp.float32)


def block_scales(block, total):
    diag = identity(PANEL) * block
    along = lax.rsqrt(jnp.sum(diag, axis=0, keepdims=True) / total + tiny)
    down = lax.rsqrt(jnp.sum(diag, axis=1, keepdims=True) / total + tiny)
    return along, down


def products_block(sums_ref, index):
    each = sums_ref.shape[0] // 4
    return sums_ref[index * each:(index + 1) * each, :SMALL].reshape(PANEL, PANEL)


def first_kernel(total, sums_ref, rest_ref, inv_ref, cross_ref):
    block = products_block(sums_ref, 0)
    along0, down0 = block_scales(block, total)
    inverse = eliminate(block * down0 * along0 / total)
    inv_ref[...] = inverse
    block = products_block(sums_ref, 2)
    along1, down1 = block_scales(block, total)
    cross = dot(inverse, products_block(sums_ref, 1) * down0 * along1 / total, (1, 0))
    cross_ref[...] = cross
    rest_ref[...] = block * down1 * along1 / total - dot(cross, cross, (0, 0))


def second_kernel(total, sums_ref, rest_ref, inv0_ref, cross_ref, out_ref):
    inv1 = eliminate(rest_ref[...])
    along0, _ = block_scales(products_block(sums_ref, 0), total)
    along1, _ = block_scales(products_block(sums_ref, 2), total)
    inv0 = inv0_ref[...]
    mixed = -dot(dot(inv1, cross_ref[...], (1, 1)), inv0, (1, 0))
    out_ref[0:PANEL, 0:PANEL] = inv0 * along0
    out_ref[0:PANEL, PANEL:] = jnp.zeros((PANEL, PANEL), jnp.float32)
    out_ref[PANEL:, 0:PANEL] = mixed * along0
    out_ref[PANEL:, PANEL:] = inv1 * along1


def call(kernel, name, outs, *args):
    shapes = [jax.ShapeDtypeStruct((k * PANEL, k * PANEL), jnp.float32) for k in outs]
    return pl.pallas_call(
        kernel,
        out_shape=shapes,
        compiler_params=pltpu.CompilerParams(vmem_limit_bytes=16 * MIB),
        name=name,
    )(*args)


def first_half(sums, total):
    return call(functools.partial(first_kernel, total), "factor_a", [1, 1, 1], sums)


def second_half(sums, rest, inv0, cross, total):
    return call(functools.partial(second_kernel, total), "factor_b", [2], sums, rest, inv0, cross)[0]


def sums_kernel(place_ref, held_ref, other_ref, matrix_ref, out_ref):
    shares = out_ref.shape[0]
    each = shares // 4
    ordered = place_ref[1] == 1
    held = held_ref[...]
    other = other_ref[...]
    panels = jnp.concatenate([jnp.where(ordered, held, other), jnp.where(ordered, other, held)], 1)
    matrix = matrix_ref[...].reshape(panels.shape[0], -1)
    products = dot(panels, jnp.concatenate([panels, matrix], 1), (0, 0))
    blocks = [products[:PANEL, :PANEL], products[:PANEL, PANEL:2 * PANEL], products[PANEL:, PANEL:2 * PANEL]]
    for i, block in enumerate(blocks):
        out_ref[i * each:(i + 1) * each, :SMALL] = block.reshape(each, SMALL, BLOCK)
    squares = jnp.sum(matrix * matrix, 0, keepdims=True)
    count = matrix.shape[1] // BLOCK
    out_ref[3 * each:, :SMALL] = jnp.zeros((shares - 3 * each, SMALL, BLOCK), jnp.float32)
    for i in range(count):
        out_ref[3 * each, i:i + 1] = squares[:, i * BLOCK:(i + 1) * BLOCK]
        block = products[:, 2 * PANEL + i * BLOCK:2 * PANEL + (i + 1) * BLOCK]
        out_ref[i * shares // count:(i + 1) * shares // count, SMALL:] = block.reshape(shares // count, -1, BLOCK)


def shared_sums(place, held, other, matrix, shares):
    columns = matrix.shape[3]
    depth = SMALL + 2 * PANEL * (columns // BLOCK) // shares
    vmem = pl.BlockSpec(memory_space=pltpu.VMEM)
    return pl.pallas_call(
        sums_kernel,
        in_specs=[pl.BlockSpec(memory_space=pltpu.SMEM), vmem, vmem, vmem],
        out_specs=vmem,
        out_shape=jax.ShapeDtypeStruct((shares, depth, BLOCK), jnp.float32),
        compiler_params=pltpu.CompilerParams(vmem_limit_bytes=48 * MIB),
        name="shared_sums",
    )(place, held, other, matrix)


def finish_kernel(total, place_ref, inv_ref, sums_ref, held_ref, other_ref, matrix_ref,
                  out_ref, growth_ref, weights_ref, factors_ref):
    count = out_ref.shape[3] // BLOCK
    place = place_ref[0]
    holder = place < 2
    wide = (1, count * BLOCK)

    @pl.when(pl.program_id(0) == 0)
    def _():
        each = sums_ref.shape[0] // count
        inverse = inv_ref[...]
        sums = [sums_ref[each * i:each * (i + 1), SMALL:].reshape(2 * PANEL, BLOCK) for i in range(count)]
        part = dot(inverse, jnp.concatenate(sums, 1), (1, 0)) / total
        subs = lax.broadcasted_iota(jnp.int32, part.shape, 0)
        lanes = lax.broadcasted_iota(jnp.int32, part.shape, 1)
        chosen = jnp.where(subs == lanes + place * PANEL, -1.0, 0.0)
        part = jnp.where(jnp.logical_and(lanes < PANEL, holder), chosen, part)
        weights = dot(inverse, part, (0, 0))
        ordered = place_ref[1] == 1
        weights_ref[:PANEL] = jnp.where(ordered, weights[:PANEL], weights[PANEL:])
        weights_ref[PANEL:] = jnp.where(ordered, weights[PANEL:], weights[:PANEL])
        place4 = 3 * sums_ref.shape[0] // 4
        squares = jnp.concatenate([sums_ref[place4, i:i + 1] for i in range(count)], 1)
        scale = jnp.sqrt(squares / total + tiny)
        growth_ref[...] = jnp.log(scale)
        in_panel = jnp.logical_and(lax.broadcasted_iota(jnp.int32, wide, 1) < PANEL, holder)
        factors_ref[0:1] = jnp.where(in_panel, 0.0, 1.0)
        factors_ref[1:2] = jnp.where(in_panel, 1.0, 1.0 / scale)

    panels = jnp.concatenate([held_ref[...], other_ref[...]], 1)
    taken = dot(panels, weights_ref[...], (1, 0))
    rows = taken.shape[0]
    block = matrix_ref[...].reshape(rows, -1)
    out_ref[...] = ((block * factors_ref[0:1] - taken) * factors_ref[1:2]).reshape(out_ref.shape)


def finish(place, inverse, sums, held, other, matrix, total):
    _, rows, sites, columns = matrix.shape
    steps = 2 if rows % 2 == 0 else 1
    block = pl.BlockSpec((1, rows // steps, sites, columns), lambda i: (i // steps, i % steps, 0, 0))
    fixed = lambda array: pl.BlockSpec(array.shape, lambda i: (0,) * array.ndim)
    panel = pl.BlockSpec((rows // steps * sites, PANEL), lambda i: (i, 0))
    return pl.pallas_call(
        functools.partial(finish_kernel, total),
        grid=(2 * steps,),
        in_specs=[
            pl.BlockSpec(memory_space=pltpu.SMEM),
            fixed(inverse),
            fixed(sums),
            panel,
            panel,
            block,
        ],
        out_specs=[block, pl.BlockSpec((1, columns), lambda i: (0, 0))],
        out_shape=[
            jax.ShapeDtypeStruct((2, rows, sites, columns), jnp.float32),
            jax.ShapeDtypeStruct((1, columns), jnp.float32),
        ],
        scratch_shapes=[
            pltpu.VMEM((2 * PANEL, columns), jnp.float32),
            pltpu.VMEM((8, columns), jnp.float32),
        ],
        compiler_params=pltpu.CompilerParams(vmem_limit_bytes=40 * MIB),
        name="finish",
    )(place, inverse, sums, held, other, matrix)


def on_device(vectors, potential):
    depth = potential.shape[0]
    _, rows, sites, columns = vectors.shape
    row_count = lax.axis_size("row")
    row_index = lax.axis_index("row")
    col_index = lax.axis_index("col")
    total = 2 * rows * sites * row_count

    col_count = lax.axis_size("col")

    def neighbours(block, cols):
        ahead = [(i * col_count + c, (i + 1) % row_count * col_count + c) for i in range(row_count) for c in cols]
        back = [(target, source) for source, target in ahead]
        return lax.ppermute(block, ("row", "col"), ahead), lax.ppermute(block, ("row", "col"), back)

    site_rows = (row_index * rows - depth + 1 + jnp.arange(rows + 2 * depth - 2)) % potential.shape[1]
    coefs = energy - site_values(jnp.take(potential, site_rows, axis=1))
    coefs = coefs.reshape(-1, sites).T
    coefs = jnp.pad(coefs, ((0, 0), (0, BLOCK - coefs.shape[1])))

    panel = vectors[..., :PANEL]
    panel = stencil(panel, *neighbours(panel, [0, 1]), coefs, depth).reshape(-1, PANEL)
    held = jnp.where(col_index < 2, panel, 0.0)
    stages = [
        [(0, 9), (1, 8)],
        [(0, 4), (8, 12), (1, 13), (9, 5)],
        [(1, 3), (13, 15), (5, 7), (9, 11), (4, 2), (0, 14), (8, 6), (12, 10)],
    ]
    for pairs in stages:
        held = held + lax.ppermute(held, "col", pairs)
    pairs = [(4, 3), (2, 1), (0, 15), (14, 13), (12, 11), (10, 9), (8, 7), (6, 5)]
    other = lax.ppermute(held, "col", pairs + [(b, a) for a, b in pairs])
    has_first = functools.reduce(jnp.logical_or, [col_index == c for c in (0, 2, 4, 5, 7, 9, 11, 14)])
    place = jnp.stack([col_index, has_first.astype(jnp.int32)])

    blocks = stencil(vectors, *neighbours(vectors, range(col_count)), coefs, depth)
    sums = lax.all_to_all(shared_sums(place, held, other, blocks, row_count), "row", 0, 0)
    share = jnp.sum(sums, 0)
    sums = lax.all_to_all(jnp.broadcast_to(share, (row_count,) + share.shape), "row", 0, 0)
    inverse = second_half(sums, *first_half(sums, total), total)
    result, growth = finish(place, inverse, sums, held, other, blocks, total)
    return (result, growth.reshape(-1))


def solution(mesh):
    return jax.shard_map(
        on_device,
        mesh=mesh,
        in_specs=(P(None, "row", None, "col"), P()),
        out_specs=(P(None, "row", None, "col"), P("col")),
        check_vma=False,
    )
```
